32 devices in a mesh: node: 16 (over z, x, core), feat: 2 (over y).
Axes of the slice: x: 2, y: 2, z: 4, core: 2. Of those that a mesh axis runs over, the one named last changes fastest.
Arguments:
- features: bfloat16 [98304, 256], P('node', 'feat'), may hold values from -6 to 6
- block_cols: int32 [768, 8], P('node', 'feat'), may hold values from 0 to 767, as said below
- tile_vals: bfloat16 [768, 8, 128, 128], P('node', 'feat'), may hold values from -0.1875 to 0.1875
- weight: bfloat16 [256, 256], replicated, may hold values from -0.375 to 0.375
- cotangent: bfloat16 [98304, 256], P('node', 'feat'), may hold values from -6 to 6
Outputs:
- activated: bfloat16 [98304, 256], P('node', 'feat')
- grad_weight: float32 [256, 256], P(None, 'feat')
- grad_feats: bfloat16 [98304, 256], P('node', 'feat')
The draws below stay inside these ranges and needn't reach their ends.
Inputs may be any that keep to these rules, and one draw needn't show every extreme that they name: `block_cols`: for each index i of node and each slot k, the block rows i * 48 to (i + 1) * 48 - 1 name in slot k at most 3 blocks of the range o * 48 to (o + 1) * 48 - 1 of any one index o, and exactly 3 of some index's range. Tiles may name the same block; their terms add.
All inputs are finite; a program needn't handle non-finite values.
Results may differ from the reference program's by a relative error of at most 0.0071.
Values may be sent and summed in bfloat16 or wider, within the bound.
A program may use at most 128 MiB of HBM per device.

```python
import math
import jax
import jax.numpy as jnp
from jax import lax

F = 256
TB = 128
KS = 8
R = 48
CAP = 3
NB = 768
NODES = 98304
N_NODE = 16
N_FEAT = 2


def one_range(key_pair):
    key_start, key_perm, key_local = jax.random.split(key_pair, 3)
    start = jax.random.randint(key_start, (), 0, N_NODE) * CAP
    positions = (start + jnp.arange(R, dtype=jnp.int32)) % (N_NODE * CAP)
    owners = positions // CAP
    owners = owners[jax.random.permutation(key_perm, R)]
    local_block = jax.random.randint(key_local, (R,), 0, R)
    return (owners * R + local_block).astype(jnp.int32)


def draw_block_cols(key, part):
    keys = jax.random.split(jax.random.fold_in(key, 17), N_NODE * KS)
    columns = jax.vmap(one_range)(keys).reshape(N_NODE, KS, R)
    return jnp.transpose(columns, (0, 2, 1)).reshape(N_NODE * R, KS)


def level_of(stream_key, dims, cuts, low, high):
    level, own = 1.0, jax.random.fold_in(stream_key, 6)
    for dim, shards_of in cuts:
        heights = jnp.exp(jax.random.uniform(jax.random.fold_in(own, dim), (shards_of,), jnp.float32, low / len(cuts), high / len(cuts)))
        level = level * jnp.repeat(heights, dims[dim] // shards_of).reshape([-1 if axis == dim else 1 for axis in range(len(dims))])
    return level


def centred(key, dims, deviation, most, cuts=(), kind=jnp.bfloat16):
    drawn = jax.random.normal(key, dims, jnp.float32) * deviation
    if len(cuts) > 0:
        drawn = level_of(key, dims, cuts, -0.22, 0.18) * drawn
    return jnp.clip(drawn, min=-most, max=most).astype(kind)


def setup_inputs(seed: int = 0) -> dict:
    splits = jax.random.split(jax.random.key(seed), 6)
    features = centred(splits[0], (NODES, F), 1.0, 6.0, ((0, 16), (1, 2)))
    block_cols = draw_block_cols(jax.random.fold_in(splits[5], 71), 0)
    tile_vals = centred(splits[2], (NB, KS, TB, TB), (TB * KS) ** -0.5, 0.1875, ((0, 16), (1, 2)))
    weight = centred(splits[3], (F, F), F ** -0.5, 0.375)
    cotangent = centred(splits[4], (NODES, F), 1.0, 6.0, ((0, 16), (1, 2)))
    return dict(features=features, block_cols=block_cols, tile_vals=tile_vals, weight=weight, cotangent=cotangent)


def reference(features, block_cols, tile_vals, weight, cotangent):
    block_count = block_cols.shape[0]
    slot_count = block_cols.shape[1]
    feat_width = features.shape[1]
    tile_size = tile_vals.shape[2]
    group_size = slot_count // N_FEAT
    block_feats = features.reshape(block_count, tile_size, feat_width).astype(jnp.float32)
    total = jnp.zeros((block_count, tile_size, feat_width), jnp.float32)
    for group_idx in range(N_FEAT):
        part_sum = jnp.zeros((block_count, tile_size, feat_width), jnp.float32)
        for inner_idx in range(group_size):
            slot_idx = group_idx * group_size + inner_idx
            source = block_feats[block_cols[:, slot_idx]]
            part_sum = part_sum + jnp.einsum('rab,rbf->raf', tile_vals[:, slot_idx].astype(jnp.float32), source)
        total = total + lax.optimization_barrier(part_sum.astype(jnp.bfloat16)).astype(jnp.float32)
    aggregate = total.reshape(block_count * tile_size, feat_width).astype(jnp.bfloat16)
    pre_act = jnp.dot(aggregate, weight, preferred_element_type=jnp.float32)
    gate_sig = jax.nn.sigmoid(pre_act)
    activated = (pre_act * gate_sig).astype(jnp.bfloat16)
    grad_pre = (cotangent.astype(jnp.float32) * gate_sig * (1.0 + pre_act * (1.0 - gate_sig))).astype(jnp.bfloat16)
    grad_weight = jnp.dot(aggregate.T, grad_pre, preferred_element_type=jnp.float32) / math.sqrt(NODES)
    grad_agg = jnp.dot(grad_pre, weight.T, preferred_element_type=jnp.float32).astype(jnp.bfloat16)
    grad_blocks = grad_agg.reshape(block_count, tile_size, feat_width).astype(jnp.float32)
    grad_total = jnp.zeros((block_count, tile_size, feat_width), jnp.float32)
    for slot_idx in range(slot_count):
        contribution = jnp.einsum('rab,raf->rbf', tile_vals[:, slot_idx].astype(jnp.float32), grad_blocks)
        contribution = lax.optimization_barrier(contribution.astype(jnp.bfloat16)).astype(jnp.float32)
        grad_total = grad_total.at[block_cols[:, slot_idx]].add(contribution)
    grad_feats = grad_total.reshape(block_count * tile_size, feat_width).astype(jnp.bfloat16)
    return (activated, grad_weight, grad_feats)
```

```python
import functools
import math

import jax
import jax.numpy as jnp
from jax import lax
from jax.experimental import pallas as pl
from jax.experimental.pallas import tpu as pltpu
from jax.sharding import PartitionSpec as P

MESH = pl.DeviceIdType.MESH
F32 = jnp.float32
BF16 = jnp.bfloat16


def ring_node(pos, core, depth):
    x = pos // depth
    z = pos * (1 - 2 * x) + x * (2 * depth - 1)
    return (z * 2 + x) * 2 + core


def ring_here(n_node):
    depth = n_node // 4
    me = lax.axis_index("node")
    core, x, z = me % 2, (me // 2) % 2, me // 4
    pos = z * (1 - 2 * x) + x * (2 * depth - 1)
    return me, core, pos, depth


def remote(src, dst, send, recv, node, feat):
    return pltpu.make_async_remote_copy(
        src_ref=src,
        dst_ref=dst,
        send_sem=send,
        recv_sem=recv,
        device_id=(node, feat),
        device_id_type=MESH,
    )


def greet(devices):
    barrier = pltpu.get_barrier_semaphore()
    for node, feat in devices:
        pl.semaphore_signal(barrier, inc=1, device_id=(node, feat), device_id_type=MESH)
    pl.semaphore_wait(barrier, len(devices))


def gather_kernel(
    n_node, feats, tiles, cols, all_feats, all_tiles, all_cols,
    ring_send, ring_recv, core_send, core_recv, own_sem, swap_send, swap_recv,
):
    me, core, pos, depth = ring_here(n_node)
    feat = lax.axis_index("feat")
    count = 2 * depth
    half = feats.shape[0] // 2
    right = ring_node((pos + 1) % count, core, depth)
    left = ring_node((pos + count - 1) % count, core, depth)
    sibling = me + 1 - 2 * core
    greet([(right, feat), (left, feat), (sibling, feat), (me, 1 - feat)])

    pending = []
    parts = swap_send.shape[0] - 1
    rows = tiles.shape[0] // parts
    for i in range(parts):
        piece = pl.ds(i * rows, rows)
        pending.append(
            remote(tiles.at[piece], all_tiles.at[piece], swap_send.at[i], swap_recv.at[i], me, 1 - feat)
        )
    pending.append(remote(cols, all_cols, swap_send.at[parts], swap_recv.at[parts], me, 1 - feat))

    targets = (right, left)
    steps = [[], []]
    for step in range(count - 1):
        for way in range(2):
            at = (pos + count - step) % count if way == 0 else (pos + step) % count
            origin = ring_node(at, core, depth)
            piece = pl.ds(way * half, half)
            src = feats.at[piece] if step == 0 else all_feats.at[origin, piece]
            if step > 0:
                steps[way][step - 1].wait_recv()
            copy = remote(
                src, all_feats.at[origin, piece],
                ring_send.at[way, step], ring_recv.at[way, step], targets[way], feat,
            )
            copy.start()
            steps[way].append(copy)
            share = remote(
                src, all_feats.at[origin, piece],
                core_send.at[way, step], core_recv.at[way, step], sibling, feat,
            )
            share.start()
            pending.append(share)
        if step == 0:
            for swap in pending[: parts + 1]:
                swap.start()
            own = pltpu.make_async_copy(feats, all_feats.at[me], own_sem)
            own.start()
    for way in range(2):
        at = (pos + 1) % count if way == 0 else (pos + count - 1) % count
        origin = ring_node(at, core, depth)
        piece = pl.ds(way * half, half)
        steps[way][count - 2].wait_recv()
        share = remote(
            all_feats.at[origin, piece], all_feats.at[origin, piece],
            core_send.at[way, count - 1], core_recv.at[way, count - 1], sibling, feat,
        )
        share.start()
        pending.append(share)
    own.wait()
    for way in range(2):
        for copy in steps[way]:
            copy.wait_send()
    for copy in pending:
        copy.wait_send()
        copy.wait_recv()


def gather_all(features, tile_vals, block_cols, n_node):
    any_space = pl.BlockSpec(memory_space=pl.ANY)
    count = n_node // 2
    dma = pltpu.SemaphoreType.DMA
    return pl.pallas_call(
        functools.partial(gather_kernel, n_node),
        out_shape=(
            jax.ShapeDtypeStruct((n_node, *features.shape), features.dtype),
            jax.ShapeDtypeStruct(tile_vals.shape, tile_vals.dtype),
            jax.ShapeDtypeStruct(block_cols.shape, block_cols.dtype),
        ),
        in_specs=[any_space] * 3,
        out_specs=[any_space] * 3,
        scratch_shapes=[
            dma((2, count - 1)), dma((2, count - 1)),
            dma((2, count)), dma((2, count)),
            dma, dma((5,)), dma((5,)),
        ],
        compiler_params=pltpu.CompilerParams(
            collective_id=0, has_side_effects=True, vmem_limit_bytes=4 << 20
        ),
        name="gather_ring",
    )(features, tile_vals, block_cols)


def scatter_kernel(
    n_node, part, out, held, own, arrived,
    own_sem, core_send, core_recv, ring_send, ring_recv,
):
    me, core, pos, depth = ring_here(n_node)
    feat = lax.axis_index("feat")
    count = 2 * depth
    half = out.shape[0] // 2
    right = ring_node((pos + 1) % count, core, depth)
    left = ring_node((pos + count - 1) % count, core, depth)
    sibling = me + 1 - 2 * core
    greet([(right, feat), (left, feat), (sibling, feat)])
    targets = (right, left)

    def target_at(way, step):
        back = (pos + 2 * count - 1 - step) % count
        return back if way == 0 else (pos + 1 + step) % count

    shares, loads = {}, {}
    for step in range(count):
        for way in range(2):
            at = target_at(way, step)
            piece = pl.ds(way * half, half)
            copy = remote(
                part.at[ring_node(at, 1 - core, depth), piece], held.at[way, step],
                core_send.at[way, step], core_recv.at[way, step], sibling, feat,
            )
            copy.start()
            shares[way, step] = copy
            load = pltpu.make_async_copy(
                part.at[ring_node(at, core, depth), piece], own.at[way, step], own_sem.at[way, step]
            )
            load.start()
            loads[way, step] = load

    chunk = 256
    sends = {}
    for step in range(count):
        for way in range(2):
            loads[way, step].wait()
            shares[way, step].wait_recv()
            if step > 0:
                sends[way, step - 1].wait_recv()

            @pl.loop(0, half // chunk)
            def _(i, way=way, step=step):
                rows = pl.ds(pl.multiple_of(i * chunk, chunk), chunk)
                total = own[way, step, rows, :].astype(F32) + held[way, step, rows, :].astype(F32)
                if step > 0:
                    total = total + arrived[way, step - 1, rows, :].astype(F32)
                if step == count - 1:
                    spot = pl.ds(pl.multiple_of(way * half + i * chunk, chunk), chunk)
                    out[spot, :] = total.astype(BF16)
                else:
                    own[way, step, rows, :] = total.astype(BF16)

            if step < count - 1:
                copy = remote(
                    own.at[way, step], arrived.at[way, step],
                    ring_send.at[way, step], ring_recv.at[way, step], targets[way], feat,
                )
                copy.start()
                sends[way, step] = copy
    for copy in shares.values():
        copy.wait_send()
    for copy in sends.values():
        copy.wait_send()


def scatter_sum(part, n_node):
    count = n_node // 2
    rows, width = part.shape[1:]
    half = rows // 2
    dma = pltpu.SemaphoreType.DMA
    return pl.pallas_call(
        functools.partial(scatter_kernel, n_node),
        out_shape=jax.ShapeDtypeStruct((rows, width), BF16),
        in_specs=[pl.BlockSpec(memory_space=pl.ANY)],
        out_specs=pl.BlockSpec(memory_space=pltpu.VMEM),
        scratch_shapes=[
            pltpu.VMEM((2, count, half, width), BF16),
            pltpu.VMEM((2, count, half, width), BF16),
            pltpu.VMEM((2, count - 1, half, width), BF16),
            dma((2, count)),
            dma((2, count)), dma((2, count)),
            dma((2, count - 1)), dma((2, count - 1)),
        ],
        compiler_params=pltpu.CompilerParams(
            collective_id=1, has_side_effects=True, vmem_limit_bytes=48 << 20
        ),
        name="scatter_ring",
    )(part)


def spread_kernel(group, cols_a, cols_b, tiles_a, tiles_b, feats, out):
    base = pl.program_id(0) * group
    for r in range(group):
        total = jnp.zeros(out.shape[1:], F32)
        for cols, tiles in ((cols_a, tiles_a), (cols_b, tiles_b)):
            for k in range(tiles.shape[1]):
                total += jnp.dot(
                    tiles[r, k], feats[cols[base + r, k]], preferred_element_type=F32
                )
        out[r] = total.astype(BF16)


def spread(cols_a, cols_b, tiles_a, tiles_b, feats):
    rows, slots, side, _ = tiles_a.shape
    blocks, _, width = feats.shape
    group = math.gcd(rows, 4)
    tile_spec = pl.BlockSpec((group, slots, side, side), lambda i, *_: (i, 0, 0, 0))
    return pl.pallas_call(
        functools.partial(spread_kernel, group),
        out_shape=jax.ShapeDtypeStruct((rows, side, width), BF16),
        grid_spec=pltpu.PrefetchScalarGridSpec(
            num_scalar_prefetch=2,
            grid=(rows // group,),
            in_specs=[
                tile_spec,
                tile_spec,
                pl.BlockSpec((blocks, side, width), lambda i, *_: (0, 0, 0), pipeline_mode=pl.Buffered(1)),
            ],
            out_specs=pl.BlockSpec((group, side, width), lambda i, *_: (i, 0, 0)),
        ),
        compiler_params=pltpu.CompilerParams(vmem_limit_bytes=40 << 20),
        cost_estimate=pl.CostEstimate(
            flops=4 * rows * slots * side * side * width,
            bytes_accessed=2 * (feats.size + 2 * tiles_a.size),
            transcendentals=0,
        ),
        name="spread",
    )(cols_a, cols_b, tiles_a, tiles_b, feats)


def collect_kernel(group, cols_a, cols_b, tiles_a, tiles_b, grads, part):
    @pl.when(pl.program_id(0) == 0)
    def _():
        @pl.loop(0, part.shape[0])
        def _(i):
            part[i] = jnp.zeros(part.shape[1:], BF16)

    base = pl.program_id(0) * group
    for r in range(group):
        for cols, tiles in ((cols_a, tiles_a), (cols_b, tiles_b)):
            for k in range(tiles.shape[1]):
                term = lax.dot_general(
                    tiles[r, k], grads[r], (((0,), (0,)), ((), ())), preferred_element_type=F32
                )
                block = cols[base + r, k]
                part[block] = (part[block].astype(F32) + term).astype(BF16)


def collect(cols_a, cols_b, tiles_a, tiles_b, grads, blocks):
    rows, slots, side, _ = tiles_a.shape
    width = grads.shape[2]
    group = math.gcd(rows, 4)
    tile_spec = pl.BlockSpec((group, slots, side, side), lambda i, *_: (i, 0, 0, 0))
    return pl.pallas_call(
        functools.partial(collect_kernel, group),
        out_shape=jax.ShapeDtypeStruct((blocks, side, width), BF16),
        grid_spec=pltpu.PrefetchScalarGridSpec(
            num_scalar_prefetch=2,
            grid=(rows // group,),
            in_specs=[
                tile_spec,
                tile_spec,
                pl.BlockSpec((group, side, width), lambda i, *_: (i, 0, 0)),
            ],
            out_specs=pl.BlockSpec((blocks, side, width), lambda i, *_: (0, 0, 0), pipeline_mode=pl.Buffered(1)),
        ),
        compiler_params=pltpu.CompilerParams(vmem_limit_bytes=40 << 20),
        cost_estimate=pl.CostEstimate(
            flops=4 * rows * slots * side * side * width,
            bytes_accessed=2 * (blocks * side * width + 2 * tiles_a.size),
            transcendentals=0,
        ),
        name="collect",
    )(cols_a, cols_b, tiles_a, tiles_b, grads)


def per_device_pair(features, block_cols, tile_vals, weight, cotangent):
    n_node = lax.axis_size("node")
    nodes, width = features.shape
    rows = block_cols.shape[0]
    side = tile_vals.shape[2]
    blocks = rows * n_node
    feat = lax.axis_index("feat")
    swap = [(0, 1), (1, 0)]

    def w_block(i, j):
        return lax.dynamic_slice(weight, (i * width, j * width), (width, width))

    def dot(a, b):
        return jnp.dot(a, b, preferred_element_type=F32)

    all_feats, tiles_b, cols_b = gather_all(features, tile_vals, block_cols, n_node)
    agg = spread(
        block_cols, cols_b, tile_vals, tiles_b, all_feats.reshape(blocks, side, width)
    ).reshape(nodes, width)
    agg_b = lax.ppermute(agg, "feat", swap)
    other = 1 - feat
    pre_act = dot(agg, w_block(feat, feat)) + dot(agg_b, w_block(other, feat))
    gate = jax.nn.sigmoid(pre_act)
    activated = (pre_act * gate).astype(BF16)
    grad_pre = (cotangent.astype(F32) * gate * (1.0 + pre_act * (1.0 - gate))).astype(BF16)
    grad_pre_b = lax.ppermute(grad_pre, "feat", swap)
    grad_agg = (
        dot(grad_pre, w_block(feat, feat).T) + dot(grad_pre_b, w_block(feat, other).T)
    ).astype(BF16)
    mine, theirs = dot(agg.T, grad_pre), dot(agg_b.T, grad_pre)
    local = jnp.where(
        feat == 0, jnp.concatenate([mine, theirs]), jnp.concatenate([theirs, mine])
    )
    grad_weight = lax.psum(local, "node") / math.sqrt(nodes * n_node)
    part = collect(
        block_cols, cols_b, tile_vals, tiles_b, grad_agg.reshape(rows, side, width), blocks
    )
    grad_feats = scatter_sum(part.reshape(n_node, nodes, width), n_node)
    return activated, grad_weight, grad_feats


def per_device(features, block_cols, tile_vals, weight, cotangent):
    nodes_dev = lax.axis_size("node")
    rows_blocks = block_cols.shape[0]
    slot_count = block_cols.shape[1]
    tile_size = tile_vals.shape[2]
    feat_width = weight.shape[0]
    col_share = features.shape[1]
    capacity = max(2, (rows_blocks + nodes_dev - 1) // nodes_dev)
    cap_all = slot_count * capacity
    spots = nodes_dev * cap_all
    col_index = lax.axis_index("feat")
    weight_cols = lax.dynamic_slice_in_dim(weight, col_index * col_share, col_share, 1)
    whole_rows = lax.all_gather(features, "feat", axis=1, tiled=True)

    flat = block_cols.reshape(-1)
    entries = jnp.arange(flat.shape[0], dtype=jnp.int32)
    owner = flat // rows_blocks
    earlier = (owner[:, None] == owner[None, :]) & (entries[None, :] < entries[:, None])
    slot_dest = owner * cap_all + jnp.sum(earlier.astype(jnp.int32), axis=1)
    placed = slot_dest[:, None] == jnp.arange(spots, dtype=jnp.int32)[None, :]
    request = jnp.sum(jnp.where(placed, (flat % rows_blocks)[:, None], 0), axis=0)
    placed = placed.astype(BF16)
    wanted = lax.all_to_all(
        request.reshape(nodes_dev, cap_all), "node", split_axis=0, concat_axis=0, tiled=True
    ).reshape(-1)
    selector = (
        wanted[:, None] == jnp.arange(rows_blocks, dtype=jnp.int32)[None, :]
    ).astype(BF16)

    def send(blocks):
        blocks = blocks.reshape(nodes_dev, cap_all, -1)
        got = lax.all_to_all(blocks, "node", split_axis=0, concat_axis=0, tiled=True)
        return got.reshape(spots, -1)

    fetched = send(jnp.dot(selector, whole_rows.reshape(rows_blocks, -1)))
    gathered = jnp.dot(placed, fetched)
    gathered = gathered.reshape(rows_blocks, slot_count, tile_size, feat_width)
    partial_value = jnp.einsum("rsab,rsbf->raf", tile_vals, gathered, preferred_element_type=F32)
    partial_value = partial_value.astype(BF16).reshape(rows_blocks * tile_size, feat_width)
    aggregate = lax.psum(partial_value, "feat").astype(F32).astype(BF16)
    pre_act = jnp.dot(aggregate, weight_cols, preferred_element_type=F32)
    gate_sig = jax.nn.sigmoid(pre_act)
    activated = (pre_act * gate_sig).astype(BF16)
    grad_pre = (
        cotangent.astype(F32) * gate_sig * (1.0 + pre_act * (1.0 - gate_sig))
    ).astype(BF16)
    local_weight = jnp.dot(aggregate.T, grad_pre, preferred_element_type=F32)
    nodes_all = rows_blocks * tile_size * nodes_dev
    grad_weight = lax.psum(local_weight, "node") / math.sqrt(nodes_all)
    grad_wide = lax.all_gather(grad_pre, "feat", axis=1, tiled=True)
    grad_agg = jnp.dot(grad_wide, weight.T, preferred_element_type=F32).astype(BF16)
    grad_agg = grad_agg.reshape(rows_blocks, tile_size, feat_width)
    contribution = jnp.einsum(
        "rsab,raf->rsbf", tile_vals, grad_agg, preferred_element_type=F32
    ).astype(BF16)
    incoming = send(jnp.dot(placed.T, contribution.reshape(flat.shape[0], -1)))
    owned_sum = jnp.dot(selector.T, incoming, preferred_element_type=F32).reshape(
        rows_blocks * tile_size, feat_width
    )
    grad_feats = lax.psum_scatter(owned_sum, "feat", scatter_dimension=1, tiled=True).astype(BF16)
    return (activated, grad_weight, grad_feats)


def solution(mesh):
    pair = mesh.shape["feat"] == 2 and mesh.shape["node"] == 16
    return jax.shard_map(
        per_device_pair if pair else per_device,
        mesh=mesh,
        in_specs=(
            P("node", "feat"),
            P("node", "feat"),
            P("node", "feat", None, None),
            P(),
            P("node", "feat"),
        ),
        out_specs=(P("node", "feat"), P(None, "feat"), P("node", "feat")),
        check_vma=False,
    )
```

```python
import functools
import math

import jax
import jax.numpy as jnp
from jax import lax
from jax.experimental import pallas as pl
from jax.experimental.pallas import tpu as pltpu
from jax.sharding import PartitionSpec as P

MESH = pl.DeviceIdType.MESH
F32 = jnp.float32
BF16 = jnp.bfloat16
STREAMS = 4


def ring_node(pos, core, depth):
    x = pos // depth
    z = pos * (1 - 2 * x) + x * (2 * depth - 1)
    return (z * 2 + x) * 2 + core


def ring_here(n_node):
    depth = n_node // 4
    me = lax.axis_index("node")
    core, x, z = me % 2, (me // 2) % 2, me // 4
    pos = z * (1 - 2 * x) + x * (2 * depth - 1)
    return me, core, pos, depth


def remote(src, dst, send, recv, node, feat):
    return pltpu.make_async_remote_copy(
        src_ref=src,
        dst_ref=dst,
        send_sem=send,
        recv_sem=recv,
        device_id=(node, feat),
        device_id_type=MESH,
    )


def greet(devices):
    barrier = pltpu.get_barrier_semaphore()
    for node, feat in devices:
        pl.semaphore_signal(barrier, inc=1, device_id=(node, feat), device_id_type=MESH)
    pl.semaphore_wait(barrier, len(devices))


def gather_kernel(
    n_node, feats, tiles, cols, all_feats, all_tiles, all_cols,
    ring_send, ring_recv, core_send, core_recv, own_sem, swap_send, swap_recv,
):
    me, core, pos, depth = ring_here(n_node)
    feat = lax.axis_index("feat")
    count = 2 * depth
    size = feats.shape[0] // STREAMS
    right = ring_node((pos + 1) % count, core, depth)
    left = ring_node((pos + count - 1) % count, core, depth)
    sibling = me + 1 - 2 * core
    greet([(right, feat), (left, feat), (sibling, feat), (me, 1 - feat)])

    pending = []
    parts = swap_send.shape[0] - 1
    rows = tiles.shape[0] // parts
    for i in range(parts):
        piece = pl.ds(i * rows, rows)
        pending.append(
            remote(tiles.at[piece], all_tiles.at[piece], swap_send.at[i], swap_recv.at[i], me, 1 - feat)
        )
    pending.append(remote(cols, all_cols, swap_send.at[parts], swap_recv.at[parts], me, 1 - feat))

    targets = (right, left)
    steps = {}
    for step in range(count):
        for j in range(STREAMS):
            way = j % 2
            at = (pos + count - step) % count if way == 0 else (pos + step) % count
            origin = ring_node(at, core, depth)
            piece = pl.ds(j * size, size)
            dst = all_feats.at[origin, piece]
            src = feats.at[piece] if step == 0 else dst
            if step > 0:
                steps[j, step - 1].wait_recv()
            if step < count - 1:
                copy = remote(
                    src, dst, ring_send.at[j, step], ring_recv.at[j, step], targets[way], feat
                )
                copy.start()
                steps[j, step] = copy
            share = remote(src, dst, core_send.at[j, step], core_recv.at[j, step], sibling, feat)
            share.start()
            pending.append(share)
        if step == 0:
            for swap in pending[: parts + 1]:
                swap.start()
            own = pltpu.make_async_copy(feats, all_feats.at[me], own_sem)
            own.start()
    own.wait()
    for copy in steps.values():
        copy.wait_send()
    for copy in pending:
        copy.wait_send()
        copy.wait_recv()


def gather_all(features, tile_vals, block_cols, n_node):
    any_space = pl.BlockSpec(memory_space=pl.ANY)
    count = n_node // 2
    dma = pltpu.SemaphoreType.DMA
    return pl.pallas_call(
        functools.partial(gather_kernel, n_node),
        out_shape=(
            jax.ShapeDtypeStruct((n_node, *features.shape), features.dtype),
            jax.ShapeDtypeStruct(tile_vals.shape, tile_vals.dtype),
            jax.ShapeDtypeStruct(block_cols.shape, block_cols.dtype),
        ),
        in_specs=[any_space] * 3,
        out_specs=[any_space] * 3,
        scratch_shapes=[
            dma((STREAMS, count - 1)), dma((STREAMS, count - 1)),
            dma((STREAMS, count)), dma((STREAMS, count)),
            dma, dma((5,)), dma((5,)),
        ],
        compiler_params=pltpu.CompilerParams(
            collective_id=0, has_side_effects=True, vmem_limit_bytes=4 << 20
        ),
        name="gather_ring",
    )(features, tile_vals, block_cols)


def scatter_kernel(
    n_node, scale, part, weight_part, out, weight_out,
    held, own, arrived, w_sib, w_slots, w_send, w_recv,
    own_sem, core_send, core_recv, ring_send, ring_recv,
):
    me, core, pos, depth = ring_here(n_node)
    feat = lax.axis_index("feat")
    count = 2 * depth
    size = out.shape[0] // STREAMS
    right = ring_node((pos + 1) % count, core, depth)
    left = ring_node((pos + count - 1) % count, core, depth)
    sibling = me + 1 - 2 * core
    greet([(right, feat), (left, feat), (sibling, feat)])
    targets = (right, left)
    streams = [(j % 2, j) for j in range(STREAMS)]

    def target_at(way, step):
        back = (pos + 2 * count - 1 - step) % count
        return back if way == 0 else (pos + 1 + step) % count

    shares, loads, sends = {}, {}, {}

    def fetch(step):
        for way, j in streams:
            at = target_at(way, step)
            piece = pl.ds(j * size, size)
            copy = remote(
                part.at[ring_node(at, 1 - core, depth), piece], held.at[j, step],
                core_send.at[j, step], core_recv.at[j, step], sibling, feat,
            )
            copy.start()
            shares[j, step] = copy
            load = pltpu.make_async_copy(
                part.at[ring_node(at, core, depth), piece], own.at[j, step], own_sem.at[j, step]
            )
            load.start()
            loads[j, step] = load

    w_rows = weight_part.shape[0] // 2
    w_mine = pl.ds(pl.multiple_of(core * w_rows, w_rows), w_rows)
    w_theirs = pl.ds(pl.multiple_of((1 - core) * w_rows, w_rows), w_rows)
    w_copies = []

    def w_copy(src, dst, node):
        i = len(w_copies)
        copy = remote(src, dst, w_send.at[i], w_recv.at[i], node, feat)
        copy.start()
        w_copies.append(copy)
        return copy

    w_ways = [[], []]
    w_lengths = (count // 2, count - 1 - count // 2)

    def weight_step(step):
        if step == 1:
            w_copies[0].wait_recv()
            w_slots[pos] = weight_part[w_mine, :] + w_sib[...]
        hop = step - 1
        for way in range(2):
            if 0 < hop <= w_lengths[way]:
                w_ways[way][hop - 1].wait_recv()
            if 0 <= hop < w_lengths[way]:
                at = (pos + count - hop) % count if way == 0 else (pos + hop) % count
                w_ways[way].append(w_copy(w_slots.at[at], w_slots.at[at], targets[way]))
        if hop == count // 2:
            total = w_slots[0]
            for i in range(1, count):
                total = total + w_slots[i]
            weight_out[w_mine, :] = total * scale
            w_copy(weight_out.at[w_mine], weight_out.at[w_mine], sibling)

    fetch(0)
    fetch(1)
    w_copy(weight_part.at[w_theirs], w_sib, sibling)
    chunk = 256
    for step in range(count):
        for way, j in streams:
            loads[j, step].wait()
            shares[j, step].wait_recv()
            if step > 0:
                sends[j, step - 1].wait_recv()

            @pl.loop(0, size // chunk)
            def _(i, j=j, step=step):
                rows = pl.ds(pl.multiple_of(i * chunk, chunk), chunk)
                total = own[j, step, rows, :].astype(F32) + held[j, step, rows, :].astype(F32)
                if step > 0:
                    total = total + arrived[j, step - 1, rows, :].astype(F32)
                if step == count - 1:
                    spot = pl.ds(pl.multiple_of(j * size + i * chunk, chunk), chunk)
                    out[spot, :] = total.astype(BF16)
                else:
                    own[j, step, rows, :] = total.astype(BF16)

            if step < count - 1:
                copy = remote(
                    own.at[j, step], arrived.at[j, step],
                    ring_send.at[j, step], ring_recv.at[j, step], targets[way], feat,
                )
                copy.start()
                sends[j, step] = copy
        if step + 2 < count:
            fetch(step + 2)
        weight_step(step)
    w_copies[-1].wait_recv()
    for copy in (*shares.values(), *sends.values(), *w_copies):
        copy.wait_send()


def scatter_sum(part, weight_part, scale, n_node):
    count = n_node // 2
    rows, width = part.shape[1:]
    size = rows // STREAMS
    w_rows = weight_part.shape[0] // 2
    dma = pltpu.SemaphoreType.DMA
    vmem = pl.BlockSpec(memory_space=pltpu.VMEM)
    return pl.pallas_call(
        functools.partial(scatter_kernel, n_node, scale),
        out_shape=(
            jax.ShapeDtypeStruct((rows, width), BF16),
            jax.ShapeDtypeStruct(weight_part.shape, F32),
        ),
        in_specs=[pl.BlockSpec(memory_space=pl.ANY), vmem],
        out_specs=(vmem, vmem),
        scratch_shapes=[
            pltpu.VMEM((STREAMS, count, size, width), BF16),
            pltpu.VMEM((STREAMS, count, size, width), BF16),
            pltpu.VMEM((STREAMS, count - 1, size, width), BF16),
            pltpu.VMEM((w_rows, width), F32),
            pltpu.VMEM((count, w_rows, width), F32),
            dma((count + 1,)), dma((count + 1,)),
            dma((STREAMS, count)),
            dma((STREAMS, count)), dma((STREAMS, count)),
            dma((STREAMS, count - 1)), dma((STREAMS, count - 1)),
        ],
        compiler_params=pltpu.CompilerParams(
            collective_id=1, has_side_effects=True, vmem_limit_bytes=48 << 20
        ),
        name="scatter_ring",
    )(part, weight_part)


def spread_kernel(group, cols_a, cols_b, tiles_a, tiles_b, feats, out):
    base = pl.program_id(0) * group
    for r in range(group):
        total = jnp.zeros(out.shape[1:], F32)
        for cols, tiles in ((cols_a, tiles_a), (cols_b, tiles_b)):
            for k in range(tiles.shape[1]):
                total += jnp.dot(
                    tiles[r, k], feats[cols[base + r, k]], preferred_element_type=F32
                )
        out[r] = total.astype(BF16)


def spread(cols_a, cols_b, tiles_a, tiles_b, feats):
    rows, slots, side, _ = tiles_a.shape
    blocks, _, width = feats.shape
    group = math.gcd(rows, 4)
    tile_spec = pl.BlockSpec((group, slots, side, side), lambda i, *_: (i, 0, 0, 0))
    return pl.pallas_call(
        functools.partial(spread_kernel, group),
        out_shape=jax.ShapeDtypeStruct((rows, side, width), BF16),
        grid_spec=pltpu.PrefetchScalarGridSpec(
            num_scalar_prefetch=2,
            grid=(rows // group,),
            in_specs=[
                tile_spec,
                tile_spec,
                pl.BlockSpec((blocks, side, width), lambda i, *_: (0, 0, 0), pipeline_mode=pl.Buffered(1)),
            ],
            out_specs=pl.BlockSpec((group, side, width), lambda i, *_: (i, 0, 0)),
        ),
        compiler_params=pltpu.CompilerParams(vmem_limit_bytes=60 << 20),
        cost_estimate=pl.CostEstimate(
            flops=4 * rows * slots * side * side * width,
            bytes_accessed=2 * (feats.size + 2 * tiles_a.size),
            transcendentals=0,
        ),
        name="spread",
    )(cols_a, cols_b, tiles_a, tiles_b, feats)


def collect_kernel(group, cols_a, cols_b, tiles_a, tiles_b, grads, part):
    @pl.when(pl.program_id(0) == 0)
    def _():
        @pl.loop(0, part.shape[0])
        def _(i):
            part[i] = jnp.zeros(part.shape[1:], BF16)

    base = pl.program_id(0) * group
    for r in range(group):
        for cols, tiles in ((cols_a, tiles_a), (cols_b, tiles_b)):
            for k in range(tiles.shape[1]):
                term = lax.dot_general(
                    tiles[r, k], grads[r], (((0,), (0,)), ((), ())), preferred_element_type=F32
                )
                block = cols[base + r, k]
                part[block] = (part[block].astype(F32) + term).astype(BF16)


def collect(cols_a, cols_b, tiles_a, tiles_b, grads, blocks):
    rows, slots, side, _ = tiles_a.shape
    width = grads.shape[2]
    group = math.gcd(rows, 4)
    tile_spec = pl.BlockSpec((group, slots, side, side), lambda i, *_: (i, 0, 0, 0))
    return pl.pallas_call(
        functools.partial(collect_kernel, group),
        out_shape=jax.ShapeDtypeStruct((blocks, side, width), BF16),
        grid_spec=pltpu.PrefetchScalarGridSpec(
            num_scalar_prefetch=2,
            grid=(rows // group,),
            in_specs=[
                tile_spec,
                tile_spec,
                pl.BlockSpec((group, side, width), lambda i, *_: (i, 0, 0)),
            ],
            out_specs=pl.BlockSpec((blocks, side, width), lambda i, *_: (0, 0, 0), pipeline_mode=pl.Buffered(1)),
        ),
        compiler_params=pltpu.CompilerParams(vmem_limit_bytes=60 << 20),
        cost_estimate=pl.CostEstimate(
            flops=4 * rows * slots * side * side * width,
            bytes_accessed=2 * (blocks * side * width + 2 * tiles_a.size),
            transcendentals=0,
        ),
        name="collect",
    )(cols_a, cols_b, tiles_a, tiles_b, grads)


def per_device_pair(features, block_cols, tile_vals, weight, cotangent):
    n_node = lax.axis_size("node")
    nodes, width = features.shape
    rows = block_cols.shape[0]
    side = tile_vals.shape[2]
    blocks = rows * n_node
    feat = lax.axis_index("feat")
    swap = [(0, 1), (1, 0)]

    def w_block(i, j):
        return lax.dynamic_slice(weight, (i * width, j * width), (width, width))

    def dot(a, b):
        return jnp.dot(a, b, preferred_element_type=F32)

    all_feats, tiles_b, cols_b = gather_all(features, tile_vals, block_cols, n_node)
    agg = spread(
        block_cols, cols_b, tile_vals, tiles_b, all_feats.reshape(blocks, side, width)
    ).reshape(nodes, width)
    agg_b = lax.ppermute(agg, "feat", swap)
    other = 1 - feat
    pre_act = dot(agg, w_block(feat, feat)) + dot(agg_b, w_block(other, feat))
    gate = jax.nn.sigmoid(pre_act)
    activated = (pre_act * gate).astype(BF16)
    grad_pre = (cotangent.astype(F32) * gate * (1.0 + pre_act * (1.0 - gate))).astype(BF16)
    grad_pre_b = lax.ppermute(grad_pre, "feat", swap)
    grad_agg = (
        dot(grad_pre, w_block(feat, feat).T) + dot(grad_pre_b, w_block(feat, other).T)
    ).astype(BF16)
    mine, theirs = dot(agg.T, grad_pre), dot(agg_b.T, grad_pre)
    local = jnp.where(
        feat == 0, jnp.concatenate([mine, theirs]), jnp.concatenate([theirs, mine])
    )
    part = collect(
        block_cols, cols_b, tile_vals, tiles_b, grad_agg.reshape(rows, side, width), blocks
    )
    grad_feats, grad_weight = scatter_sum(
        part.reshape(n_node, nodes, width), local, 1.0 / math.sqrt(nodes * n_node), n_node
    )
    return activated, grad_weight, grad_feats


def per_device(features, block_cols, tile_vals, weight, cotangent):
    nodes_dev = lax.axis_size("node")
    rows_blocks = block_cols.shape[0]
    slot_count = block_cols.shape[1]
    tile_size = tile_vals.shape[2]
    feat_width = weight.shape[0]
    col_share = features.shape[1]
    capacity = max(2, (rows_blocks + nodes_dev - 1) // nodes_dev)
    cap_all = slot_count * capacity
    spots = nodes_dev * cap_all
    col_index = lax.axis_index("feat")
    weight_cols = lax.dynamic_slice_in_dim(weight, col_index * col_share, col_share, 1)
    whole_rows = lax.all_gather(features, "feat", axis=1, tiled=True)

    flat = block_cols.reshape(-1)
    entries = jnp.arange(flat.shape[0], dtype=jnp.int32)
    owner = flat // rows_blocks
    earlier = (owner[:, None] == owner[None, :]) & (entries[None, :] < entries[:, None])
    slot_dest = owner * cap_all + jnp.sum(earlier.astype(jnp.int32), axis=1)
    placed = slot_dest[:, None] == jnp.arange(spots, dtype=jnp.int32)[None, :]
    request = jnp.sum(jnp.where(placed, (flat % rows_blocks)[:, None], 0), axis=0)
    placed = placed.astype(BF16)
    wanted = lax.all_to_all(
        request.reshape(nodes_dev, cap_all), "node", split_axis=0, concat_axis=0, tiled=True
    ).reshape(-1)
    selector = (
        wanted[:, None] == jnp.arange(rows_blocks, dtype=jnp.int32)[None, :]
    ).astype(BF16)

    def send(blocks):
        blocks = blocks.reshape(nodes_dev, cap_all, -1)
        got = lax.all_to_all(blocks, "node", split_axis=0, concat_axis=0, tiled=True)
        return got.reshape(spots, -1)

    fetched = send(jnp.dot(selector, whole_rows.reshape(rows_blocks, -1)))
    gathered = jnp.dot(placed, fetched)
    gathered = gathered.reshape(rows_blocks, slot_count, tile_size, feat_width)
    partial_value = jnp.einsum("rsab,rsbf->raf", tile_vals, gathered, preferred_element_type=F32)
    partial_value = partial_value.astype(BF16).reshape(rows_blocks * tile_size, feat_width)
    aggregate = lax.psum(partial_value, "feat").astype(F32).astype(BF16)
    pre_act = jnp.dot(aggregate, weight_cols, preferred_element_type=F32)
    gate_sig = jax.nn.sigmoid(pre_act)
    activated = (pre_act * gate_sig).astype(BF16)
    grad_pre = (
        cotangent.astype(F32) * gate_sig * (1.0 + pre_act * (1.0 - gate_sig))
    ).astype(BF16)
    local_weight = jnp.dot(aggregate.T, grad_pre, preferred_element_type=F32)
    nodes_all = rows_blocks * tile_size * nodes_dev
    grad_weight = lax.psum(local_weight, "node") / math.sqrt(nodes_all)
    grad_wide = lax.all_gather(grad_pre, "feat", axis=1, tiled=True)
    grad_agg = jnp.dot(grad_wide, weight.T, preferred_element_type=F32).astype(BF16)
    grad_agg = grad_agg.reshape(rows_blocks, tile_size, feat_width)
    contribution = jnp.einsum(
        "rsab,raf->rsbf", tile_vals, grad_agg, preferred_element_type=F32
    ).astype(BF16)
    incoming = send(jnp.dot(placed.T, contribution.reshape(flat.shape[0], -1)))
    owned_sum = jnp.dot(selector.T, incoming, preferred_element_type=F32).reshape(
        rows_blocks * tile_size, feat_width
    )
    grad_feats = lax.psum_scatter(owned_sum, "feat", scatter_dimension=1, tiled=True).astype(BF16)
    return (activated, grad_weight, grad_feats)


def solution(mesh):
    pair = mesh.shape["feat"] == 2 and mesh.shape["node"] == 16
    return jax.shard_map(
        per_device_pair if pair else per_device,
        mesh=mesh,
        in_specs=(
            P("node", "feat"),
            P("node", "feat"),
            P("node", "feat", None, None),
            P(),
            P("node", "feat"),
        ),
        out_specs=(P("node", "feat"), P(None, "feat"), P("node", "feat")),
        check_vma=False,
    )
```

```python
import functools
import math

import jax
import jax.numpy as jnp
from jax import lax
from jax.experimental import pallas as pl
from jax.experimental.pallas import tpu as pltpu
from jax.sharding import PartitionSpec as P

MESH = pl.DeviceIdType.MESH
F32 = jnp.float32
BF16 = jnp.bfloat16
STREAMS = 4


def ring_node(pos, core, depth):
    x = pos // depth
    z = pos * (1 - 2 * x) + x * (2 * depth - 1)
    return (z * 2 + x) * 2 + core


def ring_here(n_node):
    depth = n_node // 4
    me = lax.axis_index("node")
    core, x, z = me % 2, (me // 2) % 2, me // 4
    pos = z * (1 - 2 * x) + x * (2 * depth - 1)
    return me, core, pos, depth


def remote(src, dst, send, recv, node, feat):
    return pltpu.make_async_remote_copy(
        src_ref=src,
        dst_ref=dst,
        send_sem=send,
        recv_sem=recv,
        device_id=(node, feat),
        device_id_type=MESH,
    )


def greet(devices):
    barrier = pltpu.get_barrier_semaphore()
    for node, feat in devices:
        pl.semaphore_signal(barrier, inc=1, device_id=(node, feat), device_id_type=MESH)
    pl.semaphore_wait(barrier, len(devices))


def gather_kernel(
    n_node, feats, tiles, cols, cols_here, agg, agg_b, all_tiles, all_cols,
    held, tiles_a, tiles_b, cols_b, total,
    ring_send, ring_recv, core_send, core_recv, own_sem, swap_send, swap_recv,
    agg_send, agg_recv, keep_sem,
):
    me, core, pos, depth = ring_here(n_node)
    feat = lax.axis_index("feat")
    count = 2 * depth
    rows = feats.shape[0]
    size = rows // STREAMS
    right = ring_node((pos + 1) % count, core, depth)
    left = ring_node((pos + count - 1) % count, core, depth)
    sibling = me + 1 - 2 * core
    greet([(right, feat), (left, feat), (sibling, feat), (me, 1 - feat)])

    parts = swap_send.shape[0] - 1
    swaps = []
    for i in range(parts):
        piece = pl.ds(i * (rows // parts), rows // parts)
        swaps.append(
            remote(tiles.at[piece], tiles_b.at[piece], swap_send.at[i], swap_recv.at[i], me, 1 - feat)
        )
    swaps.append(remote(cols, all_cols, swap_send.at[parts], swap_recv.at[parts], me, 1 - feat))

    targets = (right, left)
    steps, shares = {}, []
    for step in range(count):
        for j in range(STREAMS):
            way = j % 2
            at = (pos + count - step) % count if way == 0 else (pos + step) % count
            dst = held.at[pl.ds(ring_node(at, core, depth) * rows + j * size, size)]
            src = feats.at[pl.ds(j * size, size)] if step == 0 else dst
            if step > 0:
                steps[j, step - 1].wait_recv()
            if step < count - 1:
                copy = remote(
                    src, dst, ring_send.at[j, step], ring_recv.at[j, step], targets[way], feat
                )
                copy.start()
                steps[j, step] = copy
            share = remote(src, dst, core_send.at[j, step], core_recv.at[j, step], sibling, feat)
            share.start()
            shares.append(share)
        if step == 0:
            for swap in swaps:
                swap.start()
            own = pltpu.make_async_copy(feats, held.at[pl.ds(me * rows, rows)], own_sem.at[0])
            own.start()
            own_tiles = pltpu.make_async_copy(tiles, tiles_a, own_sem.at[1])
            own_tiles.start()
    swaps[parts].wait_recv()
    load_cols = pltpu.make_async_copy(all_cols, cols_b, own_sem.at[2])
    load_cols.start()
    for swap in swaps[:parts]:
        swap.wait_recv()
    keep_tiles = pltpu.make_async_copy(tiles_b, all_tiles, own_sem.at[3])
    keep_tiles.start()
    for copy in (load_cols, own, own_tiles):
        copy.wait()
    for share in shares:
        share.wait_recv()

    groups = agg_send.shape[0]
    group = rows // groups
    outs = []
    for g in range(groups):

        @pl.loop(0, group // 2)
        def _(i, g=g):
            for r in (g * group + 2 * i, g * group + 2 * i + 1):
                acc = jnp.zeros(total.shape[1:], F32)
                for names, block in ((cols_here, tiles_a), (cols_b, tiles_b)):
                    for k in range(tiles.shape[1]):
                        acc += jnp.dot(block[r, k], held[names[r, k]], preferred_element_type=F32)
                total[r] = acc.astype(BF16)

        piece = pl.ds(g * group, group)
        copy = remote(
            total.at[piece], agg_b.at[piece], agg_send.at[g], agg_recv.at[g], me, 1 - feat
        )
        copy.start()
        keep = pltpu.make_async_copy(total.at[piece], agg.at[piece], keep_sem.at[g])
        keep.start()
        outs.append((copy, keep))
    for copy, keep in outs:
        keep.wait()
        copy.wait_recv()
        copy.wait_send()
    keep_tiles.wait()
    for copy in (*steps.values(), *shares, *swaps):
        copy.wait_send()


def gather_spread(features, tile_vals, block_cols, n_node):
    any_space = pl.BlockSpec(memory_space=pl.ANY)
    count = n_node // 2
    dma = pltpu.SemaphoreType.DMA
    rows = features.shape[0]
    agg = jax.ShapeDtypeStruct(features.shape, BF16)
    return pl.pallas_call(
        functools.partial(gather_kernel, n_node),
        out_shape=(
            agg,
            agg,
            jax.ShapeDtypeStruct(tile_vals.shape, tile_vals.dtype),
            jax.ShapeDtypeStruct(block_cols.shape, block_cols.dtype),
        ),
        in_specs=[any_space] * 3 + [pl.BlockSpec(memory_space=pltpu.SMEM)],
        out_specs=[any_space] * 4,
        scratch_shapes=[
            pltpu.VMEM((n_node * rows, *features.shape[1:]), BF16),
            pltpu.VMEM(tile_vals.shape, BF16),
            pltpu.VMEM(tile_vals.shape, BF16),
            pltpu.SMEM(block_cols.shape, jnp.int32),
            pltpu.VMEM(features.shape, BF16),
            dma((STREAMS, count - 1)), dma((STREAMS, count - 1)),
            dma((STREAMS, count)), dma((STREAMS, count)),
            dma((4,)), dma((5,)), dma((5,)),
            dma((4,)), dma((4,)), dma((4,)),
        ],
        compiler_params=pltpu.CompilerParams(
            collective_id=0, has_side_effects=True, vmem_limit_bytes=60 << 20
        ),
        name="gather_spread",
    )(features, tile_vals, block_cols, block_cols)


def scatter_kernel(
    n_node, scale, part, weight_part, out, weight_out,
    held, own, arrived, w_sib, w_slots, w_send, w_recv,
    own_sem, core_send, core_recv, ring_send, ring_recv,
):
    me, core, pos, depth = ring_here(n_node)
    feat = lax.axis_index("feat")
    count = 2 * depth
    size = out.shape[0] // STREAMS
    right = ring_node((pos + 1) % count, core, depth)
    left = ring_node((pos + count - 1) % count, core, depth)
    sibling = me + 1 - 2 * core
    greet([(right, feat), (left, feat), (sibling, feat)])
    targets = (right, left)
    streams = [(j % 2, j) for j in range(STREAMS)]

    def target_at(way, step):
        back = (pos + 2 * count - 1 - step) % count
        return back if way == 0 else (pos + 1 + step) % count

    shares, loads, sends = {}, {}, {}

    def fetch(step):
        for way, j in streams:
            at = target_at(way, step)
            piece = pl.ds(j * size, size)
            copy = remote(
                part.at[ring_node(at, 1 - core, depth), piece], held.at[j, step],
                core_send.at[j, step], core_recv.at[j, step], sibling, feat,
            )
            copy.start()
            shares[j, step] = copy
            load = pltpu.make_async_copy(
                part.at[ring_node(at, core, depth), piece], own.at[j, step], own_sem.at[j, step]
            )
            load.start()
            loads[j, step] = load

    w_rows = weight_part.shape[0] // 2
    w_mine = pl.ds(pl.multiple_of(core * w_rows, w_rows), w_rows)
    w_theirs = pl.ds(pl.multiple_of((1 - core) * w_rows, w_rows), w_rows)
    w_copies = []

    def w_copy(src, dst, node):
        i = len(w_copies)
        copy = remote(src, dst, w_send.at[i], w_recv.at[i], node, feat)
        copy.start()
        w_copies.append(copy)
        return copy

    w_ways = [[], []]
    w_lengths = (count // 2, count - 1 - count // 2)

    def weight_step(step):
        if step == 1:
            w_copies[0].wait_recv()
            w_slots[pos] = weight_part[w_mine, :] + w_sib[...]
        hop = step - 1
        for way in range(2):
            if 0 < hop <= w_lengths[way]:
                w_ways[way][hop - 1].wait_recv()
            if 0 <= hop < w_lengths[way]:
                at = (pos + count - hop) % count if way == 0 else (pos + hop) % count
                w_ways[way].append(w_copy(w_slots.at[at], w_slots.at[at], targets[way]))
        if hop == count // 2:
            total = w_slots[0]
            for i in range(1, count):
                total = total + w_slots[i]
            weight_out[w_mine, :] = total * scale
            w_copy(weight_out.at[w_mine], weight_out.at[w_mine], sibling)

    fetch(0)
    fetch(1)
    w_copy(weight_part.at[w_theirs], w_sib, sibling)
    chunk = 256
    for step in range(count):
        for way, j in streams:
            loads[j, step].wait()
            shares[j, step].wait_recv()
            if step > 0:
                sends[j, step - 1].wait_recv()

            @pl.loop(0, size // chunk)
            def _(i, j=j, step=step):
                rows = pl.ds(pl.multiple_of(i * chunk, chunk), chunk)
                total = own[j, step, rows, :].astype(F32) + held[j, step, rows, :].astype(F32)
                if step > 0:
                    total = total + arrived[j, step - 1, rows, :].astype(F32)
                if step == count - 1:
                    spot = pl.ds(pl.multiple_of(j * size + i * chunk, chunk), chunk)
                    out[spot, :] = total.astype(BF16)
                else:
                    own[j, step, rows, :] = total.astype(BF16)

            if step < count - 1:
                copy = remote(
                    own.at[j, step], arrived.at[j, step],
                    ring_send.at[j, step], ring_recv.at[j, step], targets[way], feat,
                )
                copy.start()
                sends[j, step] = copy
        if step + 2 < count:
            fetch(step + 2)
        weight_step(step)
    w_copies[-1].wait_recv()
    for copy in (*shares.values(), *sends.values(), *w_copies):
        copy.wait_send()


def scatter_sum(part, weight_part, scale, n_node):
    count = n_node // 2
    rows, width = part.shape[1:]
    size = rows // STREAMS
    w_rows = weight_part.shape[0] // 2
    dma = pltpu.SemaphoreType.DMA
    vmem = pl.BlockSpec(memory_space=pltpu.VMEM)
    return pl.pallas_call(
        functools.partial(scatter_kernel, n_node, scale),
        out_shape=(
            jax.ShapeDtypeStruct((rows, width), BF16),
            jax.ShapeDtypeStruct(weight_part.shape, F32),
        ),
        in_specs=[pl.BlockSpec(memory_space=pl.ANY), vmem],
        out_specs=(vmem, vmem),
        scratch_shapes=[
            pltpu.VMEM((STREAMS, count, size, width), BF16),
            pltpu.VMEM((STREAMS, count, size, width), BF16),
            pltpu.VMEM((STREAMS, count - 1, size, width), BF16),
            pltpu.VMEM((w_rows, width), F32),
            pltpu.VMEM((count, w_rows, width), F32),
            dma((count + 1,)), dma((count + 1,)),
            dma((STREAMS, count)),
            dma((STREAMS, count)), dma((STREAMS, count)),
            dma((STREAMS, count - 1)), dma((STREAMS, count - 1)),
        ],
        compiler_params=pltpu.CompilerParams(
            collective_id=1, has_side_effects=True, vmem_limit_bytes=48 << 20
        ),
        name="scatter_ring",
    )(part, weight_part)


def collect_kernel(group, cols_a, cols_b, tiles_a, tiles_b, grads, part):
    @pl.when(pl.program_id(0) == 0)
    def _():
        @pl.loop(0, part.shape[0])
        def _(i):
            part[i] = jnp.zeros(part.shape[1:], BF16)

    base = pl.program_id(0) * group
    for r in range(group):
        for cols, tiles in ((cols_a, tiles_a), (cols_b, tiles_b)):
            for k in range(tiles.shape[1]):
                term = lax.dot_general(
                    tiles[r, k], grads[r], (((0,), (0,)), ((), ())), preferred_element_type=F32
                )
                block = cols[base + r, k]
                part[block] = (part[block].astype(F32) + term).astype(BF16)


def collect(cols_a, cols_b, tiles_a, tiles_b, grads, blocks):
    rows, slots, side, _ = tiles_a.shape
    width = grads.shape[2]
    group = math.gcd(rows, 4)
    tile_spec = pl.BlockSpec((group, slots, side, side), lambda i, *_: (i, 0, 0, 0))
    return pl.pallas_call(
        functools.partial(collect_kernel, group),
        out_shape=jax.ShapeDtypeStruct((blocks, side, width), BF16),
        grid_spec=pltpu.PrefetchScalarGridSpec(
            num_scalar_prefetch=2,
            grid=(rows // group,),
            in_specs=[
                tile_spec,
                tile_spec,
                pl.BlockSpec((group, side, width), lambda i, *_: (i, 0, 0)),
            ],
            out_specs=pl.BlockSpec((blocks, side, width), lambda i, *_: (0, 0, 0), pipeline_mode=pl.Buffered(1)),
        ),
        compiler_params=pltpu.CompilerParams(vmem_limit_bytes=60 << 20),
        cost_estimate=pl.CostEstimate(
            flops=4 * rows * slots * side * side * width,
            bytes_accessed=2 * (blocks * side * width + 2 * tiles_a.size),
            transcendentals=0,
        ),
        name="collect",
    )(cols_a, cols_b, tiles_a, tiles_b, grads)


def per_device_pair(features, block_cols, tile_vals, weight, cotangent):
    n_node = lax.axis_size("node")
    nodes, width = features.shape
    rows = block_cols.shape[0]
    side = tile_vals.shape[2]
    blocks = rows * n_node
    feat = lax.axis_index("feat")
    swap = [(0, 1), (1, 0)]

    def w_block(i, j):
        return lax.dynamic_slice(weight, (i * width, j * width), (width, width))

    def dot(a, b):
        return jnp.dot(a, b, preferred_element_type=F32)

    agg, agg_b, tiles_b, cols_b = gather_spread(
        features.reshape(rows, side, width), tile_vals, block_cols, n_node
    )
    agg, agg_b = agg.reshape(nodes, width), agg_b.reshape(nodes, width)
    other = 1 - feat
    pre_act = dot(agg, w_block(feat, feat)) + dot(agg_b, w_block(other, feat))
    gate = jax.nn.sigmoid(pre_act)
    activated = (pre_act * gate).astype(BF16)
    grad_pre = (cotangent.astype(F32) * gate * (1.0 + pre_act * (1.0 - gate))).astype(BF16)
    grad_pre_b = lax.ppermute(grad_pre, "feat", swap)
    grad_agg = (
        dot(grad_pre, w_block(feat, feat).T) + dot(grad_pre_b, w_block(feat, other).T)
    ).astype(BF16)
    mine, theirs = dot(agg.T, grad_pre), dot(agg_b.T, grad_pre)
    local = jnp.where(
        feat == 0, jnp.concatenate([mine, theirs]), jnp.concatenate([theirs, mine])
    )
    part = collect(
        block_cols, cols_b, tile_vals, tiles_b, grad_agg.reshape(rows, side, width), blocks
    )
    grad_feats, grad_weight = scatter_sum(
        part.reshape(n_node, nodes, width), local, 1.0 / math.sqrt(nodes * n_node), n_node
    )
    return activated, grad_weight, grad_feats


def per_device(features, block_cols, tile_vals, weight, cotangent):
    nodes_dev = lax.axis_size("node")
    rows_blocks = block_cols.shape[0]
    slot_count = block_cols.shape[1]
    tile_size = tile_vals.shape[2]
    feat_width = weight.shape[0]
    col_share = features.shape[1]
    capacity = max(2, (rows_blocks + nodes_dev - 1) // nodes_dev)
    cap_all = slot_count * capacity
    spots = nodes_dev * cap_all
    col_index = lax.axis_index("feat")
    weight_cols = lax.dynamic_slice_in_dim(weight, col_index * col_share, col_share, 1)
    whole_rows = lax.all_gather(features, "feat", axis=1, tiled=True)

    flat = block_cols.reshape(-1)
    entries = jnp.arange(flat.shape[0], dtype=jnp.int32)
    owner = flat // rows_blocks
    earlier = (owner[:, None] == owner[None, :]) & (entries[None, :] < entries[:, None])
    slot_dest = owner * cap_all + jnp.sum(earlier.astype(jnp.int32), axis=1)
    placed = slot_dest[:, None] == jnp.arange(spots, dtype=jnp.int32)[None, :]
    request = jnp.sum(jnp.where(placed, (flat % rows_blocks)[:, None], 0), axis=0)
    placed = placed.astype(BF16)
    wanted = lax.all_to_all(
        request.reshape(nodes_dev, cap_all), "node", split_axis=0, concat_axis=0, tiled=True
    ).reshape(-1)
    selector = (
        wanted[:, None] == jnp.arange(rows_blocks, dtype=jnp.int32)[None, :]
    ).astype(BF16)

    def send(blocks):
        blocks = blocks.reshape(nodes_dev, cap_all, -1)
        got = lax.all_to_all(blocks, "node", split_axis=0, concat_axis=0, tiled=True)
        return got.reshape(spots, -1)

    fetched = send(jnp.dot(selector, whole_rows.reshape(rows_blocks, -1)))
    gathered = jnp.dot(placed, fetched)
    gathered = gathered.reshape(rows_blocks, slot_count, tile_size, feat_width)
    partial_value = jnp.einsum("rsab,rsbf->raf", tile_vals, gathered, preferred_element_type=F32)
    partial_value = partial_value.astype(BF16).reshape(rows_blocks * tile_size, feat_width)
    aggregate = lax.psum(partial_value, "feat").astype(F32).astype(BF16)
    pre_act = jnp.dot(aggregate, weight_cols, preferred_element_type=F32)
    gate_sig = jax.nn.sigmoid(pre_act)
    activated = (pre_act * gate_sig).astype(BF16)
    grad_pre = (
        cotangent.astype(F32) * gate_sig * (1.0 + pre_act * (1.0 - gate_sig))
    ).astype(BF16)
    local_weight = jnp.dot(aggregate.T, grad_pre, preferred_element_type=F32)
    nodes_all = rows_blocks * tile_size * nodes_dev
    grad_weight = lax.psum(local_weight, "node") / math.sqrt(nodes_all)
    grad_wide = lax.all_gather(grad_pre, "feat", axis=1, tiled=True)
    grad_agg = jnp.dot(grad_wide, weight.T, preferred_element_type=F32).astype(BF16)
    grad_agg = grad_agg.reshape(rows_blocks, tile_size, feat_width)
    contribution = jnp.einsum(
        "rsab,raf->rsbf", tile_vals, grad_agg, preferred_element_type=F32
    ).astype(BF16)
    incoming = send(jnp.dot(placed.T, contribution.reshape(flat.shape[0], -1)))
    owned_sum = jnp.dot(selector.T, incoming, preferred_element_type=F32).reshape(
        rows_blocks * tile_size, feat_width
    )
    grad_feats = lax.psum_scatter(owned_sum, "feat", scatter_dimension=1, tiled=True).astype(BF16)
    return (activated, grad_weight, grad_feats)


def solution(mesh):
    pair = mesh.shape["feat"] == 2 and mesh.shape["node"] == 16
    return jax.shard_map(
        per_device_pair if pair else per_device,
        mesh=mesh,
        in_specs=(
            P("node", "feat"),
            P("node", "feat"),
            P("node", "feat", None, None),
            P(),
            P("node", "feat"),
        ),
        out_specs=(P("node", "feat"), P(None, "feat"), P("node", "feat")),
        check_vma=False,
    )
```

```python
import functools
import math

import jax
import jax.numpy as jnp
from jax import lax
from jax.experimental import pallas as pl
from jax.experimental.pallas import tpu as pltpu
from jax.sharding import PartitionSpec as P

MESH = pl.DeviceIdType.MESH
F32 = jnp.float32
BF16 = jnp.bfloat16
STREAMS = 4


def ring_node(pos, core, depth):
    x = pos // depth
    z = pos * (1 - 2 * x) + x * (2 * depth - 1)
    return (z * 2 + x) * 2 + core


def ring_here(n_node):
    depth = n_node // 4
    me = lax.axis_index("node")
    core, x, z = me % 2, (me // 2) % 2, me // 4
    pos = z * (1 - 2 * x) + x * (2 * depth - 1)
    return me, core, pos, depth


def remote(src, dst, send, recv, node, feat):
    return pltpu.make_async_remote_copy(
        src_ref=src,
        dst_ref=dst,
        send_sem=send,
        recv_sem=recv,
        device_id=(node, feat),
        device_id_type=MESH,
    )


def greet(devices):
    barrier = pltpu.get_barrier_semaphore()
    for node, feat in devices:
        pl.semaphore_signal(barrier, inc=1, device_id=(node, feat), device_id_type=MESH)
    pl.semaphore_wait(barrier, len(devices))


def gather_kernel(
    n_node, feats, tiles, cols, cot, cols_here, agg, agg_b, cot_b, all_tiles, all_cols,
    held, tiles_a, tiles_b, cols_b, total,
    ring_send, ring_recv, core_send, core_recv, own_sem, swap_send, swap_recv,
    agg_send, agg_recv, keep_sem, cot_send, cot_recv,
):
    me, core, pos, depth = ring_here(n_node)
    feat = lax.axis_index("feat")
    count = 2 * depth
    rows = feats.shape[0]
    size = rows // STREAMS
    right = ring_node((pos + 1) % count, core, depth)
    left = ring_node((pos + count - 1) % count, core, depth)
    sibling = me + 1 - 2 * core
    greet([(right, feat), (left, feat), (sibling, feat), (me, 1 - feat)])

    parts = swap_send.shape[0] - 1
    swaps = []
    for i in range(parts):
        piece = pl.ds(i * (rows // parts), rows // parts)
        swaps.append(
            remote(tiles.at[piece], tiles_b.at[piece], swap_send.at[i], swap_recv.at[i], me, 1 - feat)
        )
    swaps.append(remote(cols, all_cols, swap_send.at[parts], swap_recv.at[parts], me, 1 - feat))

    part_rows = rows // 2
    mine = pl.ds(feat * part_rows, part_rows)
    theirs = pl.ds((1 - feat) * part_rows, part_rows)
    targets = (right, left)
    steps, shares = {}, []
    for step in range(count):
        for j in range(STREAMS):
            way = j % 2
            at = (pos + count - step) % count if way == 0 else (pos + step) % count
            dst = held.at[pl.ds(ring_node(at, core, depth) * rows + j * size, size)]
            src = feats.at[pl.ds(j * size, size)] if step == 0 else dst
            if step > 0:
                steps[j, step - 1].wait_recv()
            if step < count - 1:
                copy = remote(
                    src, dst, ring_send.at[j, step], ring_recv.at[j, step], targets[way], feat
                )
                copy.start()
                steps[j, step] = copy
            share = remote(src, dst, core_send.at[j, step], core_recv.at[j, step], sibling, feat)
            share.start()
            shares.append(share)
        if step == 0:
            for swap in swaps:
                swap.start()
            cot_copy = remote(cot.at[theirs], cot_b, cot_send, cot_recv, me, 1 - feat)
            cot_copy.start()
            own = pltpu.make_async_copy(feats, held.at[pl.ds(me * rows, rows)], own_sem.at[0])
            own.start()
            own_tiles = pltpu.make_async_copy(tiles, tiles_a, own_sem.at[1])
            own_tiles.start()
    swaps[parts].wait_recv()
    load_cols = pltpu.make_async_copy(all_cols, cols_b, own_sem.at[2])
    load_cols.start()
    for swap in swaps[:parts]:
        swap.wait_recv()
    keep_tiles = pltpu.make_async_copy(tiles_b, all_tiles, own_sem.at[3])
    keep_tiles.start()
    for copy in (load_cols, own, own_tiles):
        copy.wait()
    for share in shares:
        share.wait_recv()

    def multiply(first, amount):
        @pl.loop(0, amount // 2)
        def _(i):
            for r in (first + 2 * i, first + 2 * i + 1):
                acc = jnp.zeros(total.shape[1:], F32)
                for names, block in ((cols_here, tiles_a), (cols_b, tiles_b)):
                    for k in range(tiles.shape[1]):
                        acc += jnp.dot(block[r, k], held[names[r, k]], preferred_element_type=F32)
                total[r] = acc.astype(BF16)

    groups = agg_send.shape[0]
    group = part_rows // groups
    outs = []
    for g in range(groups):
        first = (1 - feat) * part_rows + g * group
        multiply(first, group)
        copy = remote(
            total.at[pl.ds(first, group)], agg_b.at[pl.ds(g * group, group)],
            agg_send.at[g], agg_recv.at[g], me, 1 - feat,
        )
        copy.start()
        outs.append(copy)
    multiply(feat * part_rows, part_rows)
    keep = pltpu.make_async_copy(total.at[mine], agg, keep_sem)
    keep.start()
    keep.wait()
    for copy in (cot_copy, *outs):
        copy.wait_recv()
        copy.wait_send()
    keep_tiles.wait()
    for copy in (*steps.values(), *shares, *swaps):
        copy.wait_send()


def gather_spread(features, tile_vals, block_cols, cotangent, n_node):
    any_space = pl.BlockSpec(memory_space=pl.ANY)
    count = n_node // 2
    dma = pltpu.SemaphoreType.DMA
    rows = features.shape[0]
    agg = jax.ShapeDtypeStruct((rows // 2, *features.shape[1:]), BF16)
    return pl.pallas_call(
        functools.partial(gather_kernel, n_node),
        out_shape=(
            agg,
            agg,
            agg,
            jax.ShapeDtypeStruct(tile_vals.shape, tile_vals.dtype),
            jax.ShapeDtypeStruct(block_cols.shape, block_cols.dtype),
        ),
        in_specs=[any_space] * 4 + [pl.BlockSpec(memory_space=pltpu.SMEM)],
        out_specs=[any_space] * 5,
        scratch_shapes=[
            pltpu.VMEM((n_node * rows, *features.shape[1:]), BF16),
            pltpu.VMEM(tile_vals.shape, BF16),
            pltpu.VMEM(tile_vals.shape, BF16),
            pltpu.SMEM(block_cols.shape, jnp.int32),
            pltpu.VMEM(features.shape, BF16),
            dma((STREAMS, count - 1)), dma((STREAMS, count - 1)),
            dma((STREAMS, count)), dma((STREAMS, count)),
            dma((4,)), dma((5,)), dma((5,)),
            dma((4,)), dma((4,)), dma, dma, dma,
        ],
        compiler_params=pltpu.CompilerParams(
            collective_id=0, has_side_effects=True, vmem_limit_bytes=60 << 20
        ),
        name="gather_spread",
    )(features, tile_vals, block_cols, cotangent, block_cols)


def scatter_kernel(
    n_node, scale, part, weight_part, out, weight_out,
    held, own, arrived, w_sib, w_slots, w_send, w_recv,
    own_sem, core_send, core_recv, ring_send, ring_recv,
):
    me, core, pos, depth = ring_here(n_node)
    feat = lax.axis_index("feat")
    count = 2 * depth
    size = out.shape[0] // STREAMS
    right = ring_node((pos + 1) % count, core, depth)
    left = ring_node((pos + count - 1) % count, core, depth)
    sibling = me + 1 - 2 * core
    greet([(right, feat), (left, feat), (sibling, feat)])
    targets = (right, left)
    streams = [(j % 2, j) for j in range(STREAMS)]

    def target_at(way, step):
        back = (pos + 2 * count - 1 - step) % count
        return back if way == 0 else (pos + 1 + step) % count

    shares, loads, sends = {}, {}, {}

    def fetch(step):
        for way, j in streams:
            at = target_at(way, step)
            piece = pl.ds(j * size, size)
            copy = remote(
                part.at[ring_node(at, 1 - core, depth), piece], held.at[j, step],
                core_send.at[j, step], core_recv.at[j, step], sibling, feat,
            )
            copy.start()
            shares[j, step] = copy
            load = pltpu.make_async_copy(
                part.at[ring_node(at, core, depth), piece], own.at[j, step], own_sem.at[j, step]
            )
            load.start()
            loads[j, step] = load

    w_rows = weight_part.shape[0] // 2
    w_mine = pl.ds(pl.multiple_of(core * w_rows, w_rows), w_rows)
    w_theirs = pl.ds(pl.multiple_of((1 - core) * w_rows, w_rows), w_rows)
    w_copies = []

    def w_copy(src, dst, node):
        i = len(w_copies)
        copy = remote(src, dst, w_send.at[i], w_recv.at[i], node, feat)
        copy.start()
        w_copies.append(copy)
        return copy

    w_ways = [[], []]
    w_lengths = (count // 2, count - 1 - count // 2)

    def weight_step(step):
        if step == 1:
            w_copies[0].wait_recv()
            w_slots[pos] = weight_part[w_mine, :] + w_sib[...]
        hop = step - 1
        for way in range(2):
            if 0 < hop <= w_lengths[way]:
                w_ways[way][hop - 1].wait_recv()
            if 0 <= hop < w_lengths[way]:
                at = (pos + count - hop) % count if way == 0 else (pos + hop) % count
                w_ways[way].append(w_copy(w_slots.at[at], w_slots.at[at], targets[way]))
        if hop == count // 2:
            total = w_slots[0]
            for i in range(1, count):
                total = total + w_slots[i]
            weight_out[w_mine, :] = total * scale
            w_copy(weight_out.at[w_mine], weight_out.at[w_mine], sibling)

    fetch(0)
    fetch(1)
    w_copy(weight_part.at[w_theirs], w_sib, sibling)
    chunk = 256
    for step in range(count):
        for way, j in streams:
            loads[j, step].wait()
            shares[j, step].wait_recv()
            if step > 0:
                sends[j, step - 1].wait_recv()

            @pl.loop(0, size // chunk)
            def _(i, j=j, step=step):
                rows = pl.ds(pl.multiple_of(i * chunk, chunk), chunk)
                total = own[j, step, rows, :].astype(F32) + held[j, step, rows, :].astype(F32)
                if step > 0:
                    total = total + arrived[j, step - 1, rows, :].astype(F32)
                if step == count - 1:
                    spot = pl.ds(pl.multiple_of(j * size + i * chunk, chunk), chunk)
                    out[spot, :] = total.astype(BF16)
                else:
                    own[j, step, rows, :] = total.astype(BF16)

            if step < count - 1:
                copy = remote(
                    own.at[j, step], arrived.at[j, step],
                    ring_send.at[j, step], ring_recv.at[j, step], targets[way], feat,
                )
                copy.start()
                sends[j, step] = copy
        if step + 2 < count:
            fetch(step + 2)
        weight_step(step)
    w_copies[-1].wait_recv()
    for copy in (*shares.values(), *sends.values(), *w_copies):
        copy.wait_send()


def scatter_sum(part, weight_part, scale, n_node):
    count = n_node // 2
    rows, width = part.shape[1:]
    size = rows // STREAMS
    w_rows = weight_part.shape[0] // 2
    dma = pltpu.SemaphoreType.DMA
    vmem = pl.BlockSpec(memory_space=pltpu.VMEM)
    return pl.pallas_call(
        functools.partial(scatter_kernel, n_node, scale),
        out_shape=(
            jax.ShapeDtypeStruct((rows, width), BF16),
            jax.ShapeDtypeStruct(weight_part.shape, F32),
        ),
        in_specs=[pl.BlockSpec(memory_space=pl.ANY), vmem],
        out_specs=(vmem, vmem),
        scratch_shapes=[
            pltpu.VMEM((STREAMS, count, size, width), BF16),
            pltpu.VMEM((STREAMS, count, size, width), BF16),
            pltpu.VMEM((STREAMS, count - 1, size, width), BF16),
            pltpu.VMEM((w_rows, width), F32),
            pltpu.VMEM((count, w_rows, width), F32),
            dma((count + 1,)), dma((count + 1,)),
            dma((STREAMS, count)),
            dma((STREAMS, count)), dma((STREAMS, count)),
            dma((STREAMS, count - 1)), dma((STREAMS, count - 1)),
        ],
        compiler_params=pltpu.CompilerParams(
            collective_id=1, has_side_effects=True, vmem_limit_bytes=48 << 20
        ),
        name="scatter_ring",
    )(part, weight_part)


def collect_kernel(group, cols_a, cols_b, tiles_a, tiles_b, grads, part):
    @pl.when(pl.program_id(0) == 0)
    def _():
        @pl.loop(0, part.shape[0])
        def _(i):
            part[i] = jnp.zeros(part.shape[1:], BF16)

    base = pl.program_id(0) * group
    for r in range(group):
        for cols, tiles in ((cols_a, tiles_a), (cols_b, tiles_b)):
            for k in range(tiles.shape[1]):
                term = lax.dot_general(
                    tiles[r, k], grads[r], (((0,), (0,)), ((), ())), preferred_element_type=F32
                )
                block = cols[base + r, k]
                part[block] = (part[block].astype(F32) + term).astype(BF16)


def collect(cols_a, cols_b, tiles_a, tiles_b, grads, blocks):
    rows, slots, side, _ = tiles_a.shape
    width = grads.shape[2]
    group = math.gcd(rows, 4)
    tile_spec = pl.BlockSpec((group, slots, side, side), lambda i, *_: (i, 0, 0, 0))
    return pl.pallas_call(
        functools.partial(collect_kernel, group),
        out_shape=jax.ShapeDtypeStruct((blocks, side, width), BF16),
        grid_spec=pltpu.PrefetchScalarGridSpec(
            num_scalar_prefetch=2,
            grid=(rows // group,),
            in_specs=[
                tile_spec,
                tile_spec,
                pl.BlockSpec((group, side, width), lambda i, *_: (i, 0, 0)),
            ],
            out_specs=pl.BlockSpec((blocks, side, width), lambda i, *_: (0, 0, 0), pipeline_mode=pl.Buffered(1)),
        ),
        compiler_params=pltpu.CompilerParams(vmem_limit_bytes=60 << 20),
        cost_estimate=pl.CostEstimate(
            flops=4 * rows * slots * side * side * width,
            bytes_accessed=2 * (blocks * side * width + 2 * tiles_a.size),
            transcendentals=0,
        ),
        name="collect",
    )(cols_a, cols_b, tiles_a, tiles_b, grads)


def per_device_pair(features, block_cols, tile_vals, weight, cotangent):
    n_node = lax.axis_size("node")
    nodes, width = features.shape
    rows = block_cols.shape[0]
    side = tile_vals.shape[2]
    blocks = rows * n_node
    feat = lax.axis_index("feat")
    swap = [(0, 1), (1, 0)]

    def dot(a, b):
        return jnp.dot(a, b, preferred_element_type=F32)

    def in_order(here, there, axis):
        return jnp.where(
            feat == 0,
            jnp.concatenate([here, there], axis),
            jnp.concatenate([there, here], axis),
        )

    def columns(array, index):
        return lax.dynamic_slice_in_dim(array, index * width, width, 1)

    other = 1 - feat
    half = nodes // 2
    agg, agg_b, cot_b, tiles_b, cols_b = gather_spread(
        features.reshape(rows, side, width), tile_vals, block_cols,
        cotangent.reshape(rows, side, width), n_node,
    )
    agg, agg_b, cot_b = (x.reshape(half, width) for x in (agg, agg_b, cot_b))
    cot = lax.dynamic_slice_in_dim(cotangent, feat * half, half, 0)
    agg, cot = in_order(agg, agg_b, 1), in_order(cot, cot_b, 1)
    pre_act = dot(agg, weight)
    gate = jax.nn.sigmoid(pre_act)
    act = (pre_act * gate).astype(BF16)
    grad_pre = (cot.astype(F32) * gate * (1.0 + pre_act * (1.0 - gate))).astype(BF16)
    grad_agg = dot(grad_pre, weight.T).astype(BF16)
    grad_agg_b = lax.ppermute(columns(grad_agg, other), "feat", swap)
    local = dot(agg.T, grad_pre)
    local = columns(local, feat) + lax.ppermute(columns(local, other), "feat", swap)
    act_there, grad_agg_b = lax.optimization_barrier((columns(act, other), grad_agg_b))
    act_b = lax.ppermute(act_there, "feat", swap)
    activated = in_order(columns(act, feat), act_b, 0)
    grad_agg = in_order(columns(grad_agg, feat), grad_agg_b, 0)
    part = collect(
        block_cols, cols_b, tile_vals, tiles_b, grad_agg.reshape(rows, side, width), blocks
    )
    grad_feats, grad_weight = scatter_sum(
        part.reshape(n_node, nodes, width), local, 1.0 / math.sqrt(nodes * n_node), n_node
    )
    return activated, grad_weight, grad_feats


def per_device(features, block_cols, tile_vals, weight, cotangent):
    nodes_dev = lax.axis_size("node")
    rows_blocks = block_cols.shape[0]
    slot_count = block_cols.shape[1]
    tile_size = tile_vals.shape[2]
    feat_width = weight.shape[0]
    col_share = features.shape[1]
    capacity = max(2, (rows_blocks + nodes_dev - 1) // nodes_dev)
    cap_all = slot_count * capacity
    spots = nodes_dev * cap_all
    col_index = lax.axis_index("feat")
    weight_cols = lax.dynamic_slice_in_dim(weight, col_index * col_share, col_share, 1)
    whole_rows = lax.all_gather(features, "feat", axis=1, tiled=True)

    flat = block_cols.reshape(-1)
    entries = jnp.arange(flat.shape[0], dtype=jnp.int32)
    owner = flat // rows_blocks
    earlier = (owner[:, None] == owner[None, :]) & (entries[None, :] < entries[:, None])
    slot_dest = owner * cap_all + jnp.sum(earlier.astype(jnp.int32), axis=1)
    placed = slot_dest[:, None] == jnp.arange(spots, dtype=jnp.int32)[None, :]
    request = jnp.sum(jnp.where(placed, (flat % rows_blocks)[:, None], 0), axis=0)
    placed = placed.astype(BF16)
    wanted = lax.all_to_all(
        request.reshape(nodes_dev, cap_all), "node", split_axis=0, concat_axis=0, tiled=True
    ).reshape(-1)
    selector = (
        wanted[:, None] == jnp.arange(rows_blocks, dtype=jnp.int32)[None, :]
    ).astype(BF16)

    def send(blocks):
        blocks = blocks.reshape(nodes_dev, cap_all, -1)
        got = lax.all_to_all(blocks, "node", split_axis=0, concat_axis=0, tiled=True)
        return got.reshape(spots, -1)

    fetched = send(jnp.dot(selector, whole_rows.reshape(rows_blocks, -1)))
    gathered = jnp.dot(placed, fetched)
    gathered = gathered.reshape(rows_blocks, slot_count, tile_size, feat_width)
    partial_value = jnp.einsum("rsab,rsbf->raf", tile_vals, gathered, preferred_element_type=F32)
    partial_value = partial_value.astype(BF16).reshape(rows_blocks * tile_size, feat_width)
    aggregate = lax.psum(partial_value, "feat").astype(F32).astype(BF16)
    pre_act = jnp.dot(aggregate, weight_cols, preferred_element_type=F32)
    gate_sig = jax.nn.sigmoid(pre_act)
    activated = (pre_act * gate_sig).astype(BF16)
    grad_pre = (
        cotangent.astype(F32) * gate_sig * (1.0 + pre_act * (1.0 - gate_sig))
    ).astype(BF16)
    local_weight = jnp.dot(aggregate.T, grad_pre, preferred_element_type=F32)
    nodes_all = rows_blocks * tile_size * nodes_dev
    grad_weight = lax.psum(local_weight, "node") / math.sqrt(nodes_all)
    grad_wide = lax.all_gather(grad_pre, "feat", axis=1, tiled=True)
    grad_agg = jnp.dot(grad_wide, weight.T, preferred_element_type=F32).astype(BF16)
    grad_agg = grad_agg.reshape(rows_blocks, tile_size, feat_width)
    contribution = jnp.einsum(
        "rsab,raf->rsbf", tile_vals, grad_agg, preferred_element_type=F32
    ).astype(BF16)
    incoming = send(jnp.dot(placed.T, contribution.reshape(flat.shape[0], -1)))
    owned_sum = jnp.dot(selector.T, incoming, preferred_element_type=F32).reshape(
        rows_blocks * tile_size, feat_width
    )
    grad_feats = lax.psum_scatter(owned_sum, "feat", scatter_dimension=1, tiled=True).astype(BF16)
    return (activated, grad_weight, grad_feats)


def solution(mesh):
    pair = mesh.shape["feat"] == 2 and mesh.shape["node"] == 16
    return jax.shard_map(
        per_device_pair if pair else per_device,
        mesh=mesh,
        in_specs=(
            P("node", "feat"),
            P("node", "feat"),
            P("node", "feat", None, None),
            P(),
            P("node", "feat"),
        ),
        out_specs=(P("node", "feat"), P(None, "feat"), P("node", "feat")),
        check_vma=False,
    )
```

```python
import functools
import math

import jax
import jax.numpy as jnp
from jax import lax
from jax.experimental import pallas as pl
from jax.experimental.pallas import tpu as pltpu
from jax.sharding import PartitionSpec as P

MESH = pl.DeviceIdType.MESH
F32 = jnp.float32
BF16 = jnp.bfloat16
STREAMS = 4


def ring_node(pos, core, depth):
    x = pos // depth
    z = pos * (1 - 2 * x) + x * (2 * depth - 1)
    return (z * 2 + x) * 2 + core


def ring_here(n_node):
    depth = n_node // 4
    me = lax.axis_index("node")
    core, x, z = me % 2, (me // 2) % 2, me // 4
    pos = z * (1 - 2 * x) + x * (2 * depth - 1)
    return me, core, pos, depth


def remote(src, dst, send, recv, node, feat):
    return pltpu.make_async_remote_copy(
        src_ref=src,
        dst_ref=dst,
        send_sem=send,
        recv_sem=recv,
        device_id=(node, feat),
        device_id_type=MESH,
    )


def greet(devices):
    barrier = pltpu.get_barrier_semaphore()
    for node, feat in devices:
        pl.semaphore_signal(barrier, inc=1, device_id=(node, feat), device_id_type=MESH)
    pl.semaphore_wait(barrier, len(devices))


def gather_kernel(
    n_node, feats, tiles, cols, cot, cols_here, agg, agg_b, cot_b, all_tiles, all_cols,
    held, tiles_a, tiles_b, cols_b, total,
    ring_send, ring_recv, core_send, core_recv, own_sem, swap_send, swap_recv,
    agg_send, agg_recv, keep_sem, cot_send, cot_recv,
):
    me, core, pos, depth = ring_here(n_node)
    feat = lax.axis_index("feat")
    count = 2 * depth
    rows = feats.shape[0]
    size = rows // STREAMS
    right = ring_node((pos + 1) % count, core, depth)
    left = ring_node((pos + count - 1) % count, core, depth)
    sibling = me + 1 - 2 * core
    greet([(right, feat), (left, feat), (sibling, feat), (me, 1 - feat)])

    parts = swap_send.shape[0] - 1
    swaps = []
    for i in range(parts):
        start = (feat if i < parts // 2 else 1 - feat) * (rows // 2)
        piece = pl.ds(start + i % (parts // 2) * (rows // parts), rows // parts)
        swaps.append(
            remote(tiles.at[piece], tiles_b.at[piece], swap_send.at[i], swap_recv.at[i], me, 1 - feat)
        )
    swaps.append(remote(cols, all_cols, swap_send.at[parts], swap_recv.at[parts], me, 1 - feat))

    part_rows = rows // 2
    mine = pl.ds(feat * part_rows, part_rows)
    theirs = pl.ds((1 - feat) * part_rows, part_rows)
    targets = (right, left)
    steps, shares = {}, []
    for step in range(count):
        for j in range(STREAMS):
            way = j % 2
            at = (pos + count - step) % count if way == 0 else (pos + step) % count
            dst = held.at[pl.ds(ring_node(at, core, depth) * rows + j * size, size)]
            src = feats.at[pl.ds(j * size, size)] if step == 0 else dst
            if step > 0:
                steps[j, step - 1].wait_recv()
            if step < count - 1:
                copy = remote(
                    src, dst, ring_send.at[j, step], ring_recv.at[j, step], targets[way], feat
                )
                copy.start()
                steps[j, step] = copy
            share = remote(src, dst, core_send.at[j, step], core_recv.at[j, step], sibling, feat)
            share.start()
            shares.append(share)
        if step == 0:
            swaps[parts].start()
            for swap in swaps[: parts // 2]:
                swap.start()
            cot_copy = remote(cot.at[theirs], cot_b, cot_send, cot_recv, me, 1 - feat)
            own = pltpu.make_async_copy(feats, held.at[pl.ds(me * rows, rows)], own_sem.at[0])
            own.start()
            own_tiles = pltpu.make_async_copy(tiles, tiles_a, own_sem.at[1])
            own_tiles.start()
        if step == 3:
            for swap in swaps[parts // 2 : parts]:
                swap.start()
        if step == count - 2:
            cot_copy.start()
    swaps[parts].wait_recv()
    load_cols = pltpu.make_async_copy(all_cols, cols_b, own_sem.at[2])
    load_cols.start()
    for swap in swaps[: parts // 2]:
        swap.wait_recv()
    for copy in (load_cols, own, own_tiles):
        copy.wait()
    for share in shares:
        share.wait_recv()

    def multiply(first, amount):
        @pl.loop(0, amount // 2)
        def _(i):
            for r in (first + 2 * i, first + 2 * i + 1):
                acc = jnp.zeros(total.shape[1:], F32)
                for names, block in ((cols_here, tiles_a), (cols_b, tiles_b)):
                    for k in range(tiles.shape[1]):
                        acc += jnp.dot(block[r, k], held[names[r, k]], preferred_element_type=F32)
                total[r] = acc.astype(BF16)

    groups = agg_send.shape[0]
    group = part_rows // groups
    outs = []
    for g in range(groups):
        first = (1 - feat) * part_rows + g * group
        multiply(first, group)
        copy = remote(
            total.at[pl.ds(first, group)], agg_b.at[pl.ds(g * group, group)],
            agg_send.at[g], agg_recv.at[g], me, 1 - feat,
        )
        copy.start()
        outs.append(copy)
    for swap in swaps[parts // 2 : parts]:
        swap.wait_recv()
    keep_tiles = pltpu.make_async_copy(tiles_b, all_tiles, own_sem.at[3])
    keep_tiles.start()
    multiply(feat * part_rows, part_rows)
    keep = pltpu.make_async_copy(total.at[mine], agg, keep_sem)
    keep.start()
    keep.wait()
    for copy in (cot_copy, *outs):
        copy.wait_recv()
        copy.wait_send()
    keep_tiles.wait()
    for copy in (*steps.values(), *shares, *swaps):
        copy.wait_send()


def gather_spread(features, tile_vals, block_cols, cotangent, n_node):
    any_space = pl.BlockSpec(memory_space=pl.ANY)
    count = n_node // 2
    dma = pltpu.SemaphoreType.DMA
    rows = features.shape[0]
    agg = jax.ShapeDtypeStruct((rows // 2, *features.shape[1:]), BF16)
    return pl.pallas_call(
        functools.partial(gather_kernel, n_node),
        out_shape=(
            agg,
            agg,
            agg,
            jax.ShapeDtypeStruct(tile_vals.shape, tile_vals.dtype),
            jax.ShapeDtypeStruct(block_cols.shape, block_cols.dtype),
        ),
        in_specs=[any_space] * 4 + [pl.BlockSpec(memory_space=pltpu.SMEM)],
        out_specs=[any_space] * 5,
        scratch_shapes=[
            pltpu.VMEM((n_node * rows, *features.shape[1:]), BF16),
            pltpu.VMEM(tile_vals.shape, BF16),
            pltpu.VMEM(tile_vals.shape, BF16),
            pltpu.SMEM(block_cols.shape, jnp.int32),
            pltpu.VMEM(features.shape, BF16),
            dma((STREAMS, count - 1)), dma((STREAMS, count - 1)),
            dma((STREAMS, count)), dma((STREAMS, count)),
            dma((4,)), dma((5,)), dma((5,)),
            dma((4,)), dma((4,)), dma, dma, dma,
        ],
        compiler_params=pltpu.CompilerParams(
            collective_id=0, has_side_effects=True, vmem_limit_bytes=60 << 20
        ),
        name="gather_spread",
    )(features, tile_vals, block_cols, cotangent, block_cols)


def scatter_kernel(
    n_node, scale, part, weight_part, out, weight_out,
    held, own, arrived, w_sib, w_slots, w_send, w_recv,
    own_sem, core_send, core_recv, ring_send, ring_recv,
):
    me, core, pos, depth = ring_here(n_node)
    feat = lax.axis_index("feat")
    count = 2 * depth
    size = out.shape[0] // STREAMS
    right = ring_node((pos + 1) % count, core, depth)
    left = ring_node((pos + count - 1) % count, core, depth)
    sibling = me + 1 - 2 * core
    greet([(right, feat), (left, feat), (sibling, feat)])
    targets = (right, left)
    streams = [(j % 2, j) for j in range(STREAMS)]

    def target_at(way, step):
        back = (pos + 2 * count - 1 - step) % count
        return back if way == 0 else (pos + 1 + step) % count

    shares, loads, sends = {}, {}, {}

    def fetch(step):
        for way, j in streams:
            at = target_at(way, step)
            piece = pl.ds(j * size, size)
            copy = remote(
                part.at[ring_node(at, 1 - core, depth), piece], held.at[j, step],
                core_send.at[j, step], core_recv.at[j, step], sibling, feat,
            )
            copy.start()
            shares[j, step] = copy
            load = pltpu.make_async_copy(
                part.at[ring_node(at, core, depth), piece], own.at[j, step], own_sem.at[j, step]
            )
            load.start()
            loads[j, step] = load

    w_rows = weight_part.shape[0] // 2
    w_mine = pl.ds(pl.multiple_of(core * w_rows, w_rows), w_rows)
    w_theirs = pl.ds(pl.multiple_of((1 - core) * w_rows, w_rows), w_rows)
    w_copies = []

    def w_copy(src, dst, node):
        i = len(w_copies)
        copy = remote(src, dst, w_send.at[i], w_recv.at[i], node, feat)
        copy.start()
        w_copies.append(copy)
        return copy

    w_ways = [[], []]
    w_lengths = (count // 2, count - 1 - count // 2)

    def weight_step(step):
        if step == 1:
            w_copies[0].wait_recv()
            w_slots[pos] = weight_part[w_mine, :] + w_sib[...]
        hop = step - 1
        for way in range(2):
            if 0 < hop <= w_lengths[way]:
                w_ways[way][hop - 1].wait_recv()
            if 0 <= hop < w_lengths[way]:
                at = (pos + count - hop) % count if way == 0 else (pos + hop) % count
                w_ways[way].append(w_copy(w_slots.at[at], w_slots.at[at], targets[way]))
        if hop == count // 2:
            total = w_slots[0]
            for i in range(1, count):
                total = total + w_slots[i]
            weight_out[w_mine, :] = total * scale
            w_copy(weight_out.at[w_mine], weight_out.at[w_mine], sibling)

    fetch(0)
    fetch(1)
    w_copy(weight_part.at[w_theirs], w_sib, sibling)
    chunk = 256
    for step in range(count):
        for way, j in streams:
            loads[j, step].wait()
            shares[j, step].wait_recv()
            if step > 0:
                sends[j, step - 1].wait_recv()

            @pl.loop(0, size // chunk)
            def _(i, j=j, step=step):
                rows = pl.ds(pl.multiple_of(i * chunk, chunk), chunk)
                total = own[j, step, rows, :].astype(F32) + held[j, step, rows, :].astype(F32)
                if step > 0:
                    total = total + arrived[j, step - 1, rows, :].astype(F32)
                if step == count - 1:
                    spot = pl.ds(pl.multiple_of(j * size + i * chunk, chunk), chunk)
                    out[spot, :] = total.astype(BF16)
                else:
                    own[j, step, rows, :] = total.astype(BF16)

            if step < count - 1:
                copy = remote(
                    own.at[j, step], arrived.at[j, step],
                    ring_send.at[j, step], ring_recv.at[j, step], targets[way], feat,
                )
                copy.start()
                sends[j, step] = copy
        if step + 2 < count:
            fetch(step + 2)
        weight_step(step)
    w_copies[-1].wait_recv()
    for copy in (*shares.values(), *sends.values(), *w_copies):
        copy.wait_send()


def scatter_sum(part, weight_part, scale, n_node):
    count = n_node // 2
    rows, width = part.shape[1:]
    size = rows // STREAMS
    w_rows = weight_part.shape[0] // 2
    dma = pltpu.SemaphoreType.DMA
    vmem = pl.BlockSpec(memory_space=pltpu.VMEM)
    return pl.pallas_call(
        functools.partial(scatter_kernel, n_node, scale),
        out_shape=(
            jax.ShapeDtypeStruct((rows, width), BF16),
            jax.ShapeDtypeStruct(weight_part.shape, F32),
        ),
        in_specs=[pl.BlockSpec(memory_space=pl.ANY), vmem],
        out_specs=(vmem, vmem),
        scratch_shapes=[
            pltpu.VMEM((STREAMS, count, size, width), BF16),
            pltpu.VMEM((STREAMS, count, size, width), BF16),
            pltpu.VMEM((STREAMS, count - 1, size, width), BF16),
            pltpu.VMEM((w_rows, width), F32),
            pltpu.VMEM((count, w_rows, width), F32),
            dma((count + 1,)), dma((count + 1,)),
            dma((STREAMS, count)),
            dma((STREAMS, count)), dma((STREAMS, count)),
            dma((STREAMS, count - 1)), dma((STREAMS, count - 1)),
        ],
        compiler_params=pltpu.CompilerParams(
            collective_id=1, has_side_effects=True, vmem_limit_bytes=48 << 20
        ),
        name="scatter_ring",
    )(part, weight_part)


def collect_kernel(group, cols_a, cols_b, tiles_a, tiles_b, grads, part):
    @pl.when(pl.program_id(0) == 0)
    def _():
        @pl.loop(0, part.shape[0])
        def _(i):
            part[i] = jnp.zeros(part.shape[1:], BF16)

    base = pl.program_id(0) * group
    for r in range(group):
        for cols, tiles in ((cols_a, tiles_a), (cols_b, tiles_b)):
            for k in range(tiles.shape[1]):
                term = lax.dot_general(
                    tiles[r, k], grads[r], (((0,), (0,)), ((), ())), preferred_element_type=F32
                )
                block = cols[base + r, k]
                part[block] = (part[block].astype(F32) + term).astype(BF16)


def collect(cols_a, cols_b, tiles_a, tiles_b, grads, blocks):
    rows, slots, side, _ = tiles_a.shape
    width = grads.shape[2]
    group = math.gcd(rows, 4)
    tile_spec = pl.BlockSpec((group, slots, side, side), lambda i, *_: (i, 0, 0, 0))
    return pl.pallas_call(
        functools.partial(collect_kernel, group),
        out_shape=jax.ShapeDtypeStruct((blocks, side, width), BF16),
        grid_spec=pltpu.PrefetchScalarGridSpec(
            num_scalar_prefetch=2,
            grid=(rows // group,),
            in_specs=[
                tile_spec,
                tile_spec,
                pl.BlockSpec((group, side, width), lambda i, *_: (i, 0, 0)),
            ],
            out_specs=pl.BlockSpec((blocks, side, width), lambda i, *_: (0, 0, 0), pipeline_mode=pl.Buffered(1)),
        ),
        compiler_params=pltpu.CompilerParams(vmem_limit_bytes=60 << 20),
        cost_estimate=pl.CostEstimate(
            flops=4 * rows * slots * side * side * width,
            bytes_accessed=2 * (blocks * side * width + 2 * tiles_a.size),
            transcendentals=0,
        ),
        name="collect",
    )(cols_a, cols_b, tiles_a, tiles_b, grads)


def per_device_pair(features, block_cols, tile_vals, weight, cotangent):
    n_node = lax.axis_size("node")
    nodes, width = features.shape
    rows = block_cols.shape[0]
    side = tile_vals.shape[2]
    blocks = rows * n_node
    feat = lax.axis_index("feat")
    swap = [(0, 1), (1, 0)]

    def dot(a, b):
        return jnp.dot(a, b, preferred_element_type=F32)

    def in_order(here, there, axis):
        return jnp.where(
            feat == 0,
            jnp.concatenate([here, there], axis),
            jnp.concatenate([there, here], axis),
        )

    def columns(array, index):
        return lax.dynamic_slice_in_dim(array, index * width, width, 1)

    other = 1 - feat
    half = nodes // 2
    agg, agg_b, cot_b, tiles_b, cols_b = gather_spread(
        features.reshape(rows, side, width), tile_vals, block_cols,
        cotangent.reshape(rows, side, width), n_node,
    )
    agg, agg_b, cot_b = (x.reshape(half, width) for x in (agg, agg_b, cot_b))
    cot = lax.dynamic_slice_in_dim(cotangent, feat * half, half, 0)
    agg, cot = in_order(agg, agg_b, 1), in_order(cot, cot_b, 1)
    pre_act = dot(agg, weight)
    gate = jax.nn.sigmoid(pre_act)
    act = (pre_act * gate).astype(BF16)
    grad_pre = (cot.astype(F32) * gate * (1.0 + pre_act * (1.0 - gate))).astype(BF16)
    grad_agg = dot(grad_pre, weight.T).astype(BF16)
    grad_agg_b = lax.ppermute(columns(grad_agg, other), "feat", swap)
    local = dot(agg.T, grad_pre)
    local = columns(local, feat) + lax.ppermute(columns(local, other), "feat", swap)
    act_there, grad_agg_b = lax.optimization_barrier((columns(act, other), grad_agg_b))
    act_b = lax.ppermute(act_there, "feat", swap)
    activated = in_order(columns(act, feat), act_b, 0)
    grad_agg = in_order(columns(grad_agg, feat), grad_agg_b, 0)
    part = collect(
        block_cols, cols_b, tile_vals, tiles_b, grad_agg.reshape(rows, side, width), blocks
    )
    grad_feats, grad_weight = scatter_sum(
        part.reshape(n_node, nodes, width), local, 1.0 / math.sqrt(nodes * n_node), n_node
    )
    return activated, grad_weight, grad_feats


def per_device(features, block_cols, tile_vals, weight, cotangent):
    nodes_dev = lax.axis_size("node")
    rows_blocks = block_cols.shape[0]
    slot_count = block_cols.shape[1]
    tile_size = tile_vals.shape[2]
    feat_width = weight.shape[0]
    col_share = features.shape[1]
    capacity = max(2, (rows_blocks + nodes_dev - 1) // nodes_dev)
    cap_all = slot_count * capacity
    spots = nodes_dev * cap_all
    col_index = lax.axis_index("feat")
    weight_cols = lax.dynamic_slice_in_dim(weight, col_index * col_share, col_share, 1)
    whole_rows = lax.all_gather(features, "feat", axis=1, tiled=True)

    flat = block_cols.reshape(-1)
    entries = jnp.arange(flat.shape[0], dtype=jnp.int32)
    owner = flat // rows_blocks
    earlier = (owner[:, None] == owner[None, :]) & (entries[None, :] < entries[:, None])
    slot_dest = owner * cap_all + jnp.sum(earlier.astype(jnp.int32), axis=1)
    placed = slot_dest[:, None] == jnp.arange(spots, dtype=jnp.int32)[None, :]
    request = jnp.sum(jnp.where(placed, (flat % rows_blocks)[:, None], 0), axis=0)
    placed = placed.astype(BF16)
    wanted = lax.all_to_all(
        request.reshape(nodes_dev, cap_all), "node", split_axis=0, concat_axis=0, tiled=True
    ).reshape(-1)
    selector = (
        wanted[:, None] == jnp.arange(rows_blocks, dtype=jnp.int32)[None, :]
    ).astype(BF16)

    def send(blocks):
        blocks = blocks.reshape(nodes_dev, cap_all, -1)
        got = lax.all_to_all(blocks, "node", split_axis=0, concat_axis=0, tiled=True)
        return got.reshape(spots, -1)

    fetched = send(jnp.dot(selector, whole_rows.reshape(rows_blocks, -1)))
    gathered = jnp.dot(placed, fetched)
    gathered = gathered.reshape(rows_blocks, slot_count, tile_size, feat_width)
    partial_value = jnp.einsum("rsab,rsbf->raf", tile_vals, gathered, preferred_element_type=F32)
    partial_value = partial_value.astype(BF16).reshape(rows_blocks * tile_size, feat_width)
    aggregate = lax.psum(partial_value, "feat").astype(F32).astype(BF16)
    pre_act = jnp.dot(aggregate, weight_cols, preferred_element_type=F32)
    gate_sig = jax.nn.sigmoid(pre_act)
    activated = (pre_act * gate_sig).astype(BF16)
    grad_pre = (
        cotangent.astype(F32) * gate_sig * (1.0 + pre_act * (1.0 - gate_sig))
    ).astype(BF16)
    local_weight = jnp.dot(aggregate.T, grad_pre, preferred_element_type=F32)
    nodes_all = rows_blocks * tile_size * nodes_dev
    grad_weight = lax.psum(local_weight, "node") / math.sqrt(nodes_all)
    grad_wide = lax.all_gather(grad_pre, "feat", axis=1, tiled=True)
    grad_agg = jnp.dot(grad_wide, weight.T, preferred_element_type=F32).astype(BF16)
    grad_agg = grad_agg.reshape(rows_blocks, tile_size, feat_width)
    contribution = jnp.einsum(
        "rsab,raf->rsbf", tile_vals, grad_agg, preferred_element_type=F32
    ).astype(BF16)
    incoming = send(jnp.dot(placed.T, contribution.reshape(flat.shape[0], -1)))
    owned_sum = jnp.dot(selector.T, incoming, preferred_element_type=F32).reshape(
        rows_blocks * tile_size, feat_width
    )
    grad_feats = lax.psum_scatter(owned_sum, "feat", scatter_dimension=1, tiled=True).astype(BF16)
    return (activated, grad_weight, grad_feats)


def solution(mesh):
    pair = mesh.shape["feat"] == 2 and mesh.shape["node"] == 16
    return jax.shard_map(
        per_device_pair if pair else per_device,
        mesh=mesh,
        in_specs=(
            P("node", "feat"),
            P("node", "feat"),
            P("node", "feat", None, None),
            P(),
            P("node", "feat"),
        ),
        out_specs=(P("node", "feat"), P(None, "feat"), P("node", "feat")),
        check_vma=False,
    )
```
